128 devices in a mesh: pair: 2 (over x_hi), day: 16 (over z, y), lag: 4 (over x_lo, core).
Axes of the slice: x: 4 (x_hi: 2, x_lo: 2; x = x_hi * 2 + x_lo), y: 4, z: 4, core: 2. Of those that a mesh axis runs over, the one named last changes fastest.
Arguments:
- corr: bfloat16 [2048, 64, 2048], P('pair', 'day', 'lag'), may hold values from -150 to 150
Outputs:
- pws_stack: float32 [2048, 2048], P('pair', 'lag')
- robust_stack: float32 [2048, 2048], P('pair', 'lag')
- day_weights: float32 [2048, 64], P('pair', 'day')
The draws below stay inside these ranges and needn't reach their ends.
All inputs are finite; a program needn't handle non-finite values.
Results may differ from the reference program's by a relative error of at most 0.00049.
Values may be sent and summed in bfloat16 or wider, within the bound.
A program may use at most 128 MiB of HBM per device.

```python
import math
import jax
import jax.numpy as jnp
from jax import lax

LAGS = 2048
ITERS = 3
PAIRS = 2048
DAYS = 64


def smooth_rows(values, width):
    extended = jnp.concatenate([values, values[..., :width]], axis=-1)
    running = jnp.cumsum(extended, axis=-1)
    leading = jnp.zeros(values.shape[:-1] + (1,), jnp.float32)
    running = jnp.concatenate([leading, running], axis=-1)
    return (running[..., width:width + LAGS] - running[..., :LAGS]) / width


def draw_corr(key, part):
    streams = jax.random.split(key, 11)
    width = max(LAGS // 32, 2)
    white = jax.random.truncated_normal(streams[0], -4.0, 4.0, (PAIRS, 3, LAGS), jnp.float32)
    smooth = smooth_rows(smooth_rows(white, width), width)
    smooth = smooth / jnp.sqrt(jnp.mean(smooth * smooth, axis=2, keepdims=True) + 1e-06)
    position = jnp.arange(LAGS, dtype=jnp.int32)
    centre = jax.random.randint(streams[1], (PAIRS, 1), 0, max(LAGS // 16, 1))
    spread = LAGS / 20.0

    def envelope(middle):
        offset = (position[None, :] - middle) % LAGS
        distance = jnp.minimum(offset, LAGS - offset).astype(jnp.float32)
        return jnp.exp(-(distance / spread) ** 2)
    signs = jnp.where(jax.random.uniform(streams[2], (PAIRS, 2), jnp.float32) < 0.5, -1.0, 1.0)
    causal = signs[:, 0:1] * envelope(centre) * (0.8 + smooth[:, 0, :])
    acausal = signs[:, 1:2] * envelope(centre + LAGS // 2) * (0.8 + smooth[:, 1, :])
    coda = 0.15 * smooth[:, 2, :]
    fraction = jax.random.uniform(streams[3], (PAIRS, 1), jnp.float32, 0.25, 0.75)
    season = jax.random.uniform(streams[4], (PAIRS, DAYS), jnp.float32) < fraction
    weight_causal = jnp.where(season, 1.0, 0.25)
    weight_acausal = jnp.where(season, 0.25, 1.0)
    signal = weight_causal[:, :, None] * causal[:, None, :] + weight_acausal[:, :, None] * acausal[:, None, :] + coda[:, None, :]
    amplitude = jnp.exp(jax.random.uniform(streams[5], (PAIRS, DAYS, 1), jnp.float32, math.log(0.05), math.log(2.0)))
    polarity = jnp.where(jax.random.uniform(streams[6], (PAIRS, DAYS, 1), jnp.float32) < 0.15, -1.0, 1.0)
    ramp = 1.0 + 2.0 * jnp.arange(DAYS, dtype=jnp.float32) / max(DAYS - 1, 1)
    day_scale = jnp.exp(jax.random.uniform(streams[7], (PAIRS, DAYS, 1), jnp.float32, math.log(0.1), math.log(3.0))) * ramp[None, :, None]
    lag_scale = jnp.exp(jax.random.uniform(streams[8], (PAIRS, 1, LAGS), jnp.float32, math.log(0.5), math.log(5.0)))
    noise = jax.random.truncated_normal(streams[10], -4.0, 4.0, (PAIRS, DAYS, LAGS), jnp.float32)
    return (amplitude * polarity * signal + 0.06 * noise * day_scale * lag_scale).astype(jnp.bfloat16)


def setup_inputs(seed: int = 0) -> dict:
    key_list = jax.random.split(jax.random.key(seed), 2)
    corr = draw_corr(jax.random.fold_in(key_list[1], 71), 0)
    return dict(corr=corr)


epsilon = 1e-06

def kernel_block(rows, cols, lags):
    offset = (cols[None, :] - rows[:, None]) % lags
    odd = offset % 2 == 1
    angle = jnp.pi * offset.astype(jnp.float32) / lags
    value = jnp.where(odd, 2.0 / lags * jnp.cos(angle) / jnp.where(odd, jnp.sin(angle), 1.0), 0.0)
    return value.astype(jnp.bfloat16)

def reference(corr):
    data = corr.astype(jnp.float32)
    norm2 = lax.optimization_barrier(jnp.sum(data * data, axis=2))
    rms = jnp.sqrt(norm2 / LAGS + epsilon)
    xn = data / rms[:, :, None]
    index = jnp.arange(LAGS, dtype=jnp.int32)
    kernel = lax.optimization_barrier(kernel_block(index, index, LAGS)).astype(jnp.float32)
    quad = jnp.dot(data.reshape(-1, LAGS), kernel, precision=lax.Precision.HIGHEST).reshape(data.shape)
    den = jnp.maximum(jnp.sqrt(data * data + quad * quad), 0.1 * rms[:, :, None])
    cosine = data / den
    sine = quad / den
    linear = lax.optimization_barrier(jnp.sum(xn, axis=1))
    csum = lax.optimization_barrier(jnp.sum(cosine, axis=1))
    ssum = lax.optimization_barrier(jnp.sum(sine, axis=1))
    pws = linear / DAYS * ((csum * csum + ssum * ssum) / (DAYS * DAYS))
    stack = pws
    weight = jnp.zeros((PAIRS, DAYS), jnp.float32)
    total = jnp.ones((PAIRS,), jnp.float32)
    for step in range(ITERS):
        msq = lax.optimization_barrier(jnp.sum(stack * stack, axis=1)) / LAGS
        normed = stack / jnp.sqrt(msq + epsilon)[:, None]
        coh = lax.optimization_barrier(jnp.sum(xn * normed[:, None, :], axis=2)) / LAGS
        res = lax.optimization_barrier(jnp.sum((xn - coh[:, :, None] * normed[:, None, :]) ** 2, axis=2)) / LAGS
        rbar = lax.optimization_barrier(jnp.sum(res, axis=1)) / DAYS
        weight = (0.1 + jnp.abs(coh)) / (res + rbar[:, None] + epsilon)
        stack = lax.optimization_barrier(jnp.sum(weight[:, :, None] * xn, axis=1))
        total = lax.optimization_barrier(jnp.sum(weight, axis=1))
    return (pws, stack / total[:, None], weight / total[:, None])
```

```python
import functools

import jax
import jax.numpy as jnp
import numpy as np
from jax import lax
from jax.experimental import pallas as pl
from jax.experimental.pallas import tpu as pltpu
from jax.sharding import PartitionSpec as P

ITERS = 3
EPS = 1e-06
HBM = pl.BlockSpec(memory_space=pl.ANY)
VMEM = pl.BlockSpec(memory_space=pltpu.VMEM)
F32 = jnp.float32


def hilbert_rows(rows, lags):
    offset = (np.arange(lags)[None, :] - np.arange(rows)[:, None]) % lags
    odd = offset % 2 == 1
    angle = np.pi * offset / lags
    value = np.where(odd, 2.0 / lags * np.cos(angle) / np.where(odd, np.sin(angle), 1.0), 0.0)
    return value.astype(np.float32).astype(jnp.bfloat16)


def peer(k, me_d, me_l):
    k = lax.rem(k * 37, 64)
    z = lax.rem(me_d // 4 + k // 16, 4)
    y = lax.rem(lax.rem(me_d, 4) + lax.rem(k // 4, 4), 4)
    x = lax.rem(me_l // 2 + lax.rem(k // 2, 2), 2)
    c = lax.rem(lax.rem(me_l, 2) + lax.rem(k, 2), 2)
    return z * 4 + y, x * 2 + c


def entry_barrier(d, l):
    barrier = pltpu.get_barrier_semaphore()

    def greet(k, carry):
        td, tl = peer(k, d, l)
        pl.semaphore_signal(barrier, inc=1, device_id={"day": td, "lag": tl})
        return carry

    lax.fori_loop(1, 64, greet, 0)
    pl.semaphore_wait(barrier, 63)


def exchange_kernel(rows, width, x_ref, o_ref, own_sem, send_sem, recv_sem):
    d = lax.axis_index("day")
    l = lax.axis_index("lag")
    entry_barrier(d, l)
    lanes = pl.ds(pl.multiple_of(l * width, width), width)

    def block(td, tl):
        return x_ref.at[pl.ds(pl.multiple_of((td * 4 + tl) * rows, rows), rows), :]

    def send(k, carry):
        td, tl = peer(k, d, l)
        pltpu.make_async_remote_copy(
            src_ref=block(td, tl),
            dst_ref=o_ref.at[d, :, lanes],
            send_sem=send_sem,
            recv_sem=recv_sem,
            device_id={"day": td, "lag": tl},
        ).start()
        return carry

    lax.fori_loop(1, 64, send, 0)
    own = pltpu.make_async_copy(block(d, l), o_ref.at[d, :, lanes], recv_sem)
    own.start()
    pltpu.make_async_copy(o_ref, o_ref, recv_sem).wait()
    most = x_ref.at[pl.ds(0, 63 * rows), :]
    pltpu.make_async_copy(most, most, send_sem).wait()


def exchange(x):
    total, width = x.shape
    rows = total // 64
    return pl.pallas_call(
        functools.partial(exchange_kernel, rows, width),
        out_shape=jax.ShapeDtypeStruct((16, rows, 4 * width), x.dtype),
        in_specs=[HBM],
        out_specs=HBM,
        scratch_shapes=[pltpu.SemaphoreType.DMA] * 3,
        compiler_params=pltpu.CompilerParams(collective_id=0, has_side_effects=True),
        name="exchange",
    )(x)


def group4(x):
    n = x.shape[0]
    row = lax.broadcasted_iota(jnp.int32, x.shape, 0)
    other = jnp.where(row % 2 == 0, pltpu.roll(x, n - 1, 0), pltpu.roll(x, 1, 0))
    x = x + other
    other = jnp.where(row % 4 < 2, pltpu.roll(x, n - 2, 0), pltpu.roll(x, 2, 0))
    return x + other


def stack_kernel(g_ref, x_ref, pws_ref, rob_ref, w_ref, k_ref, xn_ref, st_ref, cs_ref, ss_ref, rms_ref, coh_ref, wt_ref):
    ndev, rows, lags = x_ref.shape
    days = ndev * 4
    step = g_ref.shape[0]
    zero = jnp.zeros((rows, 128), F32)

    def lanes(x):
        return jnp.broadcast_to(jnp.sum(x, axis=1, keepdims=True), (rows, 128))

    def wide(x):
        return jnp.concatenate([x] * (lags // 128), axis=1)

    @pl.when(pl.program_id(0) == 0)
    def _():
        for i in range(lags // step):
            cut = i * step
            if cut:
                k_ref[cut:cut + step, :cut] = g_ref[:, lags - cut:]
            k_ref[cut:cut + step, cut:] = g_ref[:, :lags - cut]

    st_ref[...] = jnp.zeros((rows, lags), F32)

    @pl.loop(0, ndev)
    def _(d):
        data = x_ref[d].astype(F32)
        rms = jnp.sqrt(lanes(data * data) / lags + EPS)
        inv = 1.0 / rms
        rms_ref[d] = 10.0 * inv
        xn = data * wide(inv)
        xn_ref[d] = xn
        st_ref[...] += xn

    tile = 256

    @pl.loop(0, lags // tile)
    def _(t):
        at = pl.ds(pl.multiple_of(t * tile, tile), tile)
        quad = jnp.dot(x_ref[...].reshape(ndev * rows, lags), k_ref[:, at], preferred_element_type=F32)
        csum = jnp.zeros((rows, tile), F32)
        ssum = jnp.zeros((rows, tile), F32)
        for d in range(ndev):
            data = x_ref[d, :, at].astype(F32)
            q = quad[d * rows:(d + 1) * rows]
            top = rms_ref[d]
            inv = jnp.minimum(lax.rsqrt(data * data + q * q), jnp.concatenate([top, top], axis=1))
            csum = csum + data * inv
            ssum = ssum + q * inv
        csum = group4(csum)
        ssum = group4(ssum)
        lin = group4(st_ref[:, at])
        st_ref[:, at] = lin / days * ((csum * csum + ssum * ssum) / (days * days))

    pws_ref[...] = st_ref[...]
    for _ in range(ITERS):
        stack = st_ref[...]
        msq = lanes(stack * stack) / lags
        st_ref[...] = stack * wide(1.0 / jnp.sqrt(msq + EPS))

        def fit(d, rbar):
            coh = lanes(xn_ref[d] * st_ref[...]) / lags
            diff = xn_ref[d] - wide(coh) * st_ref[...]
            res = lanes(diff * diff) / lags
            coh_ref[d] = coh
            wt_ref[d] = res
            return rbar + res

        rbar = lax.fori_loop(0, ndev, fit, zero)
        rbar = group4(rbar) / days
        st_ref[...] = jnp.zeros((rows, lags), F32)

        def mix(d, total):
            weight = (0.1 + jnp.abs(coh_ref[d])) / (wt_ref[d] + rbar + EPS)
            wt_ref[d] = weight
            st_ref[...] += wide(weight) * xn_ref[d]
            return total + weight

        total = group4(lax.fori_loop(0, ndev, mix, zero))
        st_ref[...] = group4(st_ref[...])
    rob_ref[...] = st_ref[...] * wide(1.0 / total)
    lane = lax.broadcasted_iota(jnp.int32, (rows, 128), 1)
    w_ref[...] = lax.fori_loop(0, ndev, lambda d, w: jnp.where(lane == d, wt_ref[d] / total, w), zero)


def stacks(g, recv):
    ndev, rows, lags = recv.shape
    part = 16
    row = pl.BlockSpec((part, lags), lambda i: (i, 0))
    out = jax.ShapeDtypeStruct((rows, lags), F32)
    wide = pltpu.VMEM((part, lags), F32)
    thin = pltpu.VMEM((ndev, part, 128), F32)
    return pl.pallas_call(
        stack_kernel,
        out_shape=(out, out, jax.ShapeDtypeStruct((rows, 128), F32)),
        grid=(rows // part,),
        in_specs=[pl.BlockSpec(g.shape, lambda i: (0, 0)), pl.BlockSpec((ndev, part, lags), lambda i: (0, i, 0))],
        out_specs=(row, row, pl.BlockSpec((part, 128), lambda i: (i, 0))),
        scratch_shapes=[
            pltpu.VMEM((lags, lags), jnp.bfloat16),
            pltpu.VMEM((ndev, part, lags), F32),
            wide, wide, wide, thin, thin, thin,
        ],
        compiler_params=pltpu.CompilerParams(vmem_limit_bytes=48 * 2**20),
        name="stacks",
    )(g, recv)


def spread_kernel(rows, pws_ref, rob_ref, w_ref, pws_out, rob_out, w_out, send_sems, recv_sems):
    d = lax.axis_index("day")
    l = lax.axis_index("lag")
    entry_barrier(d, l)
    mine = d * 4 + l
    at = pl.ds(pl.multiple_of(mine * rows, rows), rows)

    def pairs(td, tl):
        yield pws_ref.at[tl], pws_out.at[at, :]
        yield rob_ref.at[tl], rob_out.at[at, :]
        yield w_ref.at[td], w_out.at[mine]

    def send(k, carry):
        td, tl = peer(k, d, l)
        for i, (src, dst) in enumerate(pairs(td, tl)):
            pltpu.make_async_remote_copy(
                src_ref=src, dst_ref=dst, send_sem=send_sems.at[i], recv_sem=recv_sems.at[i],
                device_id={"day": td, "lag": tl},
            ).start()
        return carry

    lax.fori_loop(1, 64, send, 0)
    for i, (src, dst) in enumerate(pairs(d, l)):
        pltpu.make_async_copy(src, dst, recv_sems.at[i]).start()
    for i, out in enumerate((pws_out, rob_out, w_out)):
        pltpu.make_async_copy(out, out, recv_sems.at[i]).wait()
    for i, most in enumerate((pws_out.at[pl.ds(0, 63 * rows)], rob_out.at[pl.ds(0, 63 * rows)], w_out.at[pl.ds(0, 63)])):
        pltpu.make_async_copy(most, most, send_sems.at[i]).wait()


def spread(pws, rob, w):
    _, rows, width = pws.shape
    out = jax.ShapeDtypeStruct((64 * rows, width), F32)
    return pl.pallas_call(
        functools.partial(spread_kernel, rows),
        out_shape=(out, out, jax.ShapeDtypeStruct((64,) + w.shape[1:], F32)),
        in_specs=[HBM] * 3,
        out_specs=(HBM,) * 3,
        scratch_shapes=[pltpu.SemaphoreType.DMA((3,)), pltpu.SemaphoreType.DMA((3,))],
        compiler_params=pltpu.CompilerParams(collective_id=1, has_side_effects=True),
        name="spread",
    )(pws, rob, w)


def per_device(corr):
    pairs, days_here, width = corr.shape
    lags = width * 4
    g = jnp.asarray(hilbert_rows(256, lags))
    recv = exchange(corr.reshape(pairs * days_here, width))
    pws, rob, w = stacks(g, recv)
    pws = pws[::4].reshape(16, 4, width).transpose(1, 0, 2)
    rob = rob[::4].reshape(16, 4, width).transpose(1, 0, 2)
    w = jnp.broadcast_to(w[:, :16].T.reshape(16, 1, 64), (16, 8, 64))
    w = jnp.concatenate([w, jnp.zeros_like(w)], axis=2)
    pws, rob, w = spread(pws, rob, w)
    return pws, rob, w[:, 0, :64].reshape(pairs, days_here)


def solution(mesh):
    return jax.shard_map(
        per_device,
        mesh=mesh,
        in_specs=(P("pair", "day", "lag"),),
        out_specs=(P("pair", "lag"), P("pair", "lag"), P("pair", "day")),
        check_vma=False,
    )
```

```python
import functools

import jax
import jax.numpy as jnp
import numpy as np
from jax import lax
from jax.experimental import pallas as pl
from jax.experimental.pallas import tpu as pltpu
from jax.sharding import PartitionSpec as P

ITERS = 3
EPS = 1e-06
HBM = pl.BlockSpec(memory_space=pl.ANY)
VMEM = pl.BlockSpec(memory_space=pltpu.VMEM)
F32 = jnp.float32


def hilbert_rows(rows, lags):
    offset = (np.arange(lags)[None, :] - np.arange(rows)[:, None]) % lags
    odd = offset % 2 == 1
    angle = np.pi * offset / lags
    value = np.where(odd, 2.0 / lags * np.cos(angle) / np.where(odd, np.sin(angle), 1.0), 0.0)
    return value.astype(np.float32).astype(jnp.bfloat16)


def peer(k, me_d, me_l):
    a = lax.rem(k, 4)
    z = lax.rem(me_d // 4 + a, 4)
    y = lax.rem(lax.rem(me_d, 4) + a + k // 4, 4)
    x = lax.rem(me_l // 2 + a + k // 16, 2)
    c = lax.rem(me_l + k // 32, 2)
    return z * 4 + y, x * 2 + c


def entry_barrier(d, l):
    barrier = pltpu.get_barrier_semaphore()

    def greet(k, carry):
        td, tl = peer(k, d, l)
        pl.semaphore_signal(barrier, inc=1, device_id={"day": td, "lag": tl})
        return carry

    lax.fori_loop(1, 64, greet, 0)
    pl.semaphore_wait(barrier, 63)


def group4(x):
    n = x.shape[0]
    row = lax.broadcasted_iota(jnp.int32, x.shape, 0)
    other = jnp.where(row % 2 == 0, pltpu.roll(x, n - 1, 0), pltpu.roll(x, 1, 0))
    x = x + other
    other = jnp.where(row % 4 < 2, pltpu.roll(x, n - 2, 0), pltpu.roll(x, 2, 0))
    return x + other


def wide(x, lanes):
    return jnp.concatenate([x] * (lanes // 128), axis=1)


def fold(x):
    total = x[:, :128]
    for j in range(128, x.shape[1], 128):
        total = total + x[:, j:j + 128]
    return total


def lane_sum(ref):
    ndev, rows, lanes = ref.shape
    total = jnp.sum(ref[...].reshape(ndev * rows, lanes), axis=1, keepdims=True)
    return jnp.broadcast_to(total, (ndev * rows, lanes)).reshape(ndev, rows, lanes)


def day_sum(x):
    total = x[0]
    for d in range(1, x.shape[0]):
        total = total + x[d]
    return group4(total)


def stack_kernel(parts, g_ref, x_ref, pws_ref, rob_ref, w_ref,
                 recv, k_ref, xb_ref, x32_ref, st_ref, part_ref, inv_ref, coh_ref, wt_ref, send_sem, recv_sems):
    me_d = lax.axis_index("day")
    me_l = lax.axis_index("lag")
    ndev, quads, here, lags = recv.shape[1:]
    rows = quads * here
    days = ndev * here
    width = lags // 4
    entry_barrier(me_d, me_l)
    lanes = pl.ds(pl.multiple_of(me_l * width, width), width)

    def block(r, td, tl):
        return x_ref.at[pl.ds(((td * 4 + tl) * parts + r) * quads, quads)]

    for r in range(parts):
        def send(k, carry):
            td, tl = peer(k, me_d, me_l)
            pltpu.make_async_remote_copy(
                src_ref=block(r, td, tl),
                dst_ref=recv.at[r, me_d, :, :, lanes],
                send_sem=send_sem,
                recv_sem=recv_sems.at[r],
                device_id={"day": td, "lag": tl},
            ).start()
            return carry

        lax.fori_loop(1, 64, send, 0)
        pltpu.make_async_copy(block(r, me_d, me_l), recv.at[r, me_d, :, :, lanes], recv_sems.at[r]).start()

    step = g_ref.shape[0]
    for i in range(lags // step):
        cut = i * step
        if cut:
            k_ref[cut:cut + step, :cut] = g_ref[:, lags - cut:]
        k_ref[cut:cut + step, cut:] = g_ref[:, :lags - cut]

    def one_part(r, carry):
        pltpu.make_async_copy(recv.at[r], recv.at[r], recv_sems.at[r]).wait()

        @pl.loop(0, ndev, unroll=2)
        def _(d):
            x = recv[r, d].reshape(rows, lags)
            xb_ref[d] = x
            data = x.astype(F32)
            x32_ref[d] = data
            part_ref[d] = fold(data * data)

        inv_ref[...] = 1.0 / jnp.sqrt(lane_sum(part_ref) / lags + EPS)
        tile = 256

        @pl.loop(0, lags // tile, unroll=2)
        def _(t):
            at = pl.ds(pl.multiple_of(t * tile, tile), tile)
            quad = jnp.dot(xb_ref[...].reshape(ndev * rows, lags), k_ref[:, at], preferred_element_type=F32)
            lin = jnp.zeros((rows, tile), F32)
            csum = jnp.zeros((rows, tile), F32)
            ssum = jnp.zeros((rows, tile), F32)
            for d in range(ndev):
                data = x32_ref[d, :, at]
                q = quad[d * rows:(d + 1) * rows]
                scale = wide(inv_ref[d], tile)
                inv = jnp.minimum(lax.rsqrt(data * data + q * q), 10.0 * scale)
                lin = lin + data * scale
                csum = csum + data * inv
                ssum = ssum + q * inv
            csum = group4(csum)
            ssum = group4(ssum)
            st_ref[:, at] = group4(lin) / days * ((csum * csum + ssum * ssum) / (days * days))

        out = pl.ds(pl.multiple_of(r * rows, rows), rows)
        pws_ref[out, :] = st_ref[...]
        for step in range(ITERS):
            stack = st_ref[...]
            msq = jnp.sum(fold(stack * stack), axis=1, keepdims=True) / lags
            st_ref[...] = stack * (1.0 / jnp.sqrt(msq + EPS))

            @pl.loop(0, ndev, unroll=4)
            def _(d):
                part_ref[d] = fold(x32_ref[d] * st_ref[...])

            coh_ref[...] = lane_sum(part_ref) * inv_ref[...] / lags

            @pl.loop(0, ndev, unroll=4)
            def _(d):
                diff = x32_ref[d] * wide(inv_ref[d], lags) - wide(coh_ref[d], lags) * st_ref[...]
                part_ref[d] = fold(diff * diff)

            res = lane_sum(part_ref) / lags
            rbar = day_sum(res) / days
            weight = (0.1 + jnp.abs(coh_ref[...])) / (res + rbar + EPS)
            total = day_sum(weight)
            wt_ref[...] = weight * inv_ref[...]
            chunk = 512

            @pl.loop(0, lags // chunk)
            def _(t):
                at = pl.ds(pl.multiple_of(t * chunk, chunk), chunk)
                mix = wide(wt_ref[0], chunk) * x32_ref[0, :, at]
                for d in range(1, ndev):
                    mix = mix + wide(wt_ref[d], chunk) * x32_ref[d, :, at]
                st_ref[:, at] = group4(mix)

            if step == ITERS - 1:
                rob_ref[out, :] = st_ref[...] * wide(1.0 / total, lags)
                lane = lax.broadcasted_iota(jnp.int32, (rows, 128), 1)
                shares = jnp.zeros((rows, 128), F32)
                for d in range(ndev):
                    shares = jnp.where(lane == d, weight[d] / total, shares)
                w_ref[out, :] = shares
        return carry

    lax.fori_loop(0, parts, one_part, 0)
    for r in range(parts):
        most = x_ref.at[pl.ds(0, 63 * quads)]
        pltpu.make_async_copy(most, most, send_sem).wait()


def stacks(g, x):
    pairs, here, width = x.shape
    lags = 4 * width
    parts = 4
    quads = pairs // 64 // parts
    rows = pairs // 64 * here
    part = quads * here
    out = jax.ShapeDtypeStruct((rows, lags), F32)
    thin = pltpu.VMEM((16, part, 128), F32)
    return pl.pallas_call(
        functools.partial(stack_kernel, parts),
        out_shape=(out, out, jax.ShapeDtypeStruct((rows, 128), F32)),
        in_specs=[VMEM, HBM],
        out_specs=(VMEM,) * 3,
        scratch_shapes=[
            pltpu.VMEM((parts, 16, quads, here, lags), x.dtype),
            pltpu.VMEM((lags, lags), jnp.bfloat16),
            pltpu.VMEM((16, part, lags), jnp.bfloat16),
            pltpu.VMEM((16, part, lags), F32),
            pltpu.VMEM((part, lags), F32),
            thin, thin, thin, thin,
            pltpu.SemaphoreType.DMA,
            pltpu.SemaphoreType.DMA((parts,)),
        ],
        compiler_params=pltpu.CompilerParams(collective_id=0, has_side_effects=True, vmem_limit_bytes=50 * 2**20),
        name="stacks",
    )(g, x)


def spread_kernel(rows, pws_ref, rob_ref, w_ref, pws_out, rob_out, w_out, send_sems, recv_sems):
    d = lax.axis_index("day")
    l = lax.axis_index("lag")
    entry_barrier(d, l)
    mine = d * 4 + l
    at = pl.ds(pl.multiple_of(mine * rows, rows), rows)

    def pairs(td, tl):
        yield pws_ref.at[tl], pws_out.at[at, :]
        yield rob_ref.at[tl], rob_out.at[at, :]
        yield w_ref.at[td], w_out.at[mine]

    def send(k, carry):
        td, tl = peer(k, d, l)
        for i, (src, dst) in enumerate(pairs(td, tl)):
            pltpu.make_async_remote_copy(
                src_ref=src, dst_ref=dst, send_sem=send_sems.at[i], recv_sem=recv_sems.at[i],
                device_id={"day": td, "lag": tl},
            ).start()
        return carry

    lax.fori_loop(1, 64, send, 0)
    for i, (src, dst) in enumerate(pairs(d, l)):
        pltpu.make_async_copy(src, dst, recv_sems.at[i]).start()
    for i, out in enumerate((pws_out, rob_out, w_out)):
        pltpu.make_async_copy(out, out, recv_sems.at[i]).wait()
    for i, most in enumerate((pws_out.at[pl.ds(0, 63 * rows)], rob_out.at[pl.ds(0, 63 * rows)], w_out.at[pl.ds(0, 63)])):
        pltpu.make_async_copy(most, most, send_sems.at[i]).wait()


def spread(pws, rob, w):
    _, rows, width = pws.shape
    out = jax.ShapeDtypeStruct((64 * rows, width), F32)
    return pl.pallas_call(
        functools.partial(spread_kernel, rows),
        out_shape=(out, out, jax.ShapeDtypeStruct((64,) + w.shape[1:], F32)),
        in_specs=[HBM] * 3,
        out_specs=(HBM,) * 3,
        scratch_shapes=[pltpu.SemaphoreType.DMA((3,)), pltpu.SemaphoreType.DMA((3,))],
        compiler_params=pltpu.CompilerParams(collective_id=1, has_side_effects=True),
        name="spread",
    )(pws, rob, w)


def per_device(corr):
    pairs, days_here, width = corr.shape
    lags = width * 4
    g = jnp.asarray(hilbert_rows(256, lags))
    pws, rob, w = stacks(g, corr)
    pws = pws[::4].reshape(16, 4, width).transpose(1, 0, 2)
    rob = rob[::4].reshape(16, 4, width).transpose(1, 0, 2)
    w = jnp.broadcast_to(w[:, :16].T.reshape(16, 1, 64), (16, 8, 64))
    w = jnp.concatenate([w, jnp.zeros_like(w)], axis=2)
    pws, rob, w = spread(pws, rob, w)
    return pws, rob, w[:, 0, :64].reshape(pairs, days_here)


def solution(mesh):
    return jax.shard_map(
        per_device,
        mesh=mesh,
        in_specs=(P("pair", "day", "lag"),),
        out_specs=(P("pair", "lag"), P("pair", "lag"), P("pair", "day")),
        check_vma=False,
    )
```

```python
import functools

import jax
import jax.numpy as jnp
import numpy as np
from jax import lax
from jax.experimental import pallas as pl
from jax.experimental.pallas import tpu as pltpu
from jax.sharding import PartitionSpec as P

ITERS = 3
EPS = 1e-06
HBM = pl.BlockSpec(memory_space=pl.ANY)
VMEM = pl.BlockSpec(memory_space=pltpu.VMEM)
F32 = jnp.float32


def hilbert_rows(rows, lags):
    offset = (np.arange(lags)[None, :] - np.arange(rows)[:, None]) % lags
    odd = offset % 2 == 1
    angle = np.pi * offset / lags
    value = np.where(odd, 2.0 / lags * np.cos(angle) / np.where(odd, np.sin(angle), 1.0), 0.0)
    return value.astype(np.float32).astype(jnp.bfloat16)


def peer(k, me_d, me_l):
    a = lax.rem(k, 4)
    z = lax.rem(me_d // 4 + a, 4)
    y = lax.rem(lax.rem(me_d, 4) + a + k // 4, 4)
    x = lax.rem(me_l // 2 + a + k // 16, 2)
    c = lax.rem(me_l + k // 32, 2)
    return z * 4 + y, x * 2 + c


def entry_barrier(d, l):
    barrier = pltpu.get_barrier_semaphore()

    def greet(k, carry):
        td, tl = peer(k, d, l)
        pl.semaphore_signal(barrier, inc=1, device_id={"day": td, "lag": tl})
        return carry

    lax.fori_loop(1, 64, greet, 0)
    pl.semaphore_wait(barrier, 63)


def group4(x):
    n = x.shape[0]
    row = lax.broadcasted_iota(jnp.int32, x.shape, 0)
    other = jnp.where(row % 2 == 0, pltpu.roll(x, n - 1, 0), pltpu.roll(x, 1, 0))
    x = x + other
    other = jnp.where(row % 4 < 2, pltpu.roll(x, n - 2, 0), pltpu.roll(x, 2, 0))
    return x + other


def wide(x, lanes):
    return jnp.concatenate([x] * (lanes // 128), axis=1)


def fold(x):
    total = x[:, :128]
    for j in range(128, x.shape[1], 128):
        total = total + x[:, j:j + 128]
    return total


def lane_sum(ref):
    ndev, rows, lanes = ref.shape
    total = jnp.sum(ref[...].reshape(ndev * rows, lanes), axis=1, keepdims=True)
    return jnp.broadcast_to(total, (ndev * rows, lanes)).reshape(ndev, rows, lanes)


def day_sum(x):
    total = x[0]
    for d in range(1, x.shape[0]):
        total = total + x[d]
    return group4(total)


def stack_kernel(parts, g_ref, x_ref, pws_ref, rob_ref, w_ref,
                 recv, k_ref, xb_ref, x32_ref, st_ref, part_ref, inv_ref, coh_ref, wt_ref, share_ref,
                 send_sem, recv_sems):
    me_d = lax.axis_index("day")
    me_l = lax.axis_index("lag")
    ndev, quads, here, lags = recv.shape[1:]
    rows = quads * here
    days = ndev * here
    width = lags // 4
    entry_barrier(me_d, me_l)
    lanes = pl.ds(pl.multiple_of(me_l * width, width), width)

    def block(r, td, tl):
        return x_ref.at[pl.ds(((td * 4 + tl) * parts + r) * quads, quads)]

    for r in range(parts):
        def send(k, carry):
            td, tl = peer(k, me_d, me_l)
            pltpu.make_async_remote_copy(
                src_ref=block(r, td, tl),
                dst_ref=recv.at[r, me_d, :, :, lanes],
                send_sem=send_sem,
                recv_sem=recv_sems.at[r],
                device_id={"day": td, "lag": tl},
            ).start()
            return carry

        lax.fori_loop(1, 64, send, 0)
        pltpu.make_async_copy(block(r, me_d, me_l), recv.at[r, me_d, :, :, lanes], recv_sems.at[r]).start()

    step = g_ref.shape[0]
    for i in range(lags // step):
        cut = i * step
        if cut:
            k_ref[cut:cut + step, :cut] = g_ref[:, lags - cut:]
        k_ref[cut:cut + step, cut:] = g_ref[:, :lags - cut]

    def one_part(r, carry):
        pltpu.make_async_copy(recv.at[r], recv.at[r], recv_sems.at[r]).wait()

        @pl.loop(0, ndev, unroll=2)
        def _(d):
            x = recv[r, d].reshape(rows, lags)
            xb_ref[d] = x
            data = x.astype(F32)
            x32_ref[d] = data
            part_ref[d] = fold(data * data)

        inv_ref[...] = 1.0 / jnp.sqrt(lane_sum(part_ref) / lags + EPS)
        tile = 256

        @pl.loop(0, lags // tile, unroll=2)
        def _(t):
            at = pl.ds(pl.multiple_of(t * tile, tile), tile)
            quad = jnp.dot(xb_ref[...].reshape(ndev * rows, lags), k_ref[:, at], preferred_element_type=F32)
            lin = jnp.zeros((rows, tile), F32)
            csum = jnp.zeros((rows, tile), F32)
            ssum = jnp.zeros((rows, tile), F32)
            for d in range(ndev):
                data = x32_ref[d, :, at]
                q = quad[d * rows:(d + 1) * rows]
                scale = wide(inv_ref[d], tile)
                inv = jnp.minimum(lax.rsqrt(data * data + q * q), 10.0 * scale)
                lin = lin + data * scale
                csum = csum + data * inv
                ssum = ssum + q * inv
            csum = group4(csum)
            ssum = group4(ssum)
            st_ref[:, at] = group4(lin) / days * ((csum * csum + ssum * ssum) / (days * days))

        out = pl.ds(pl.multiple_of(r * rows, rows), rows)
        pws_ref[out, :] = st_ref[...]
        for step in range(ITERS):
            stack = st_ref[...]
            msq = jnp.sum(fold(stack * stack), axis=1, keepdims=True) / lags
            st_ref[...] = stack * (1.0 / jnp.sqrt(msq + EPS))

            @pl.loop(0, ndev, unroll=4)
            def _(d):
                part_ref[d] = fold(x32_ref[d] * st_ref[...])

            coh_ref[...] = lane_sum(part_ref) * inv_ref[...] / lags

            @pl.loop(0, ndev, unroll=4)
            def _(d):
                diff = x32_ref[d] * wide(inv_ref[d], lags) - wide(coh_ref[d], lags) * st_ref[...]
                part_ref[d] = fold(diff * diff)

            res = lane_sum(part_ref) / lags
            rbar = day_sum(res) / days
            weight = (0.1 + jnp.abs(coh_ref[...])) / (res + rbar + EPS)
            total = day_sum(weight)
            wt_ref[...] = weight * inv_ref[...]
            chunk = 512

            @pl.loop(0, lags // chunk)
            def _(t):
                at = pl.ds(pl.multiple_of(t * chunk, chunk), chunk)
                mix = wide(wt_ref[0], chunk) * x32_ref[0, :, at]
                for d in range(1, ndev):
                    mix = mix + wide(wt_ref[d], chunk) * x32_ref[d, :, at]
                st_ref[:, at] = group4(mix)

            if step == ITERS - 1:
                rob_ref[out, :] = st_ref[...] * wide(1.0 / total, lags)
                lane = lax.broadcasted_iota(jnp.int32, (rows, 128), 1)
                shares = jnp.zeros((rows, 128), F32)
                for d in range(ndev):
                    shares = jnp.where(lane == d, weight[d] / total, shares)
                share_ref[out, :] = shares
        return carry

    lax.fori_loop(0, parts, one_part, 0)
    units = []
    for ref in (pws_ref, rob_ref):
        top = jnp.max(jnp.abs(ref[...]), axis=(0, 1), keepdims=True)
        top = jnp.maximum(top, 1e-30)
        ref[...] = ref[...] * (16384.0 / top)
        units.append(jnp.broadcast_to(top / 16384.0, (1, 128)))
    shares = share_ref[...].T
    lane = lax.broadcasted_iota(jnp.int32, (1, 128), 1)
    for d in range(ndev):
        row = jnp.where(lane == 64, units[0], shares[d:d + 1])
        w_ref[d] = jnp.where(lane == 65, units[1], row)
    for r in range(parts):
        most = x_ref.at[pl.ds(0, 63 * quads)]
        pltpu.make_async_copy(most, most, send_sem).wait()


def stacks(g, x):
    pairs, here, width = x.shape
    lags = 4 * width
    parts = 4
    quads = pairs // 64 // parts
    rows = pairs // 64 * here
    part = quads * here
    out = jax.ShapeDtypeStruct((rows, lags), F32)
    thin = pltpu.VMEM((16, part, 128), F32)
    return pl.pallas_call(
        functools.partial(stack_kernel, parts),
        out_shape=(out, out, jax.ShapeDtypeStruct((16, 1, 128), F32)),
        in_specs=[VMEM, HBM],
        out_specs=(VMEM,) * 3,
        scratch_shapes=[
            pltpu.VMEM((parts, 16, quads, here, lags), x.dtype),
            pltpu.VMEM((lags, lags), jnp.bfloat16),
            pltpu.VMEM((16, part, lags), jnp.bfloat16),
            pltpu.VMEM((16, part, lags), F32),
            pltpu.VMEM((part, lags), F32),
            thin, thin, thin, thin,
            pltpu.VMEM((128, 128), F32),
            pltpu.SemaphoreType.DMA,
            pltpu.SemaphoreType.DMA((parts,)),
        ],
        compiler_params=pltpu.CompilerParams(collective_id=0, has_side_effects=True, vmem_limit_bytes=50 * 2**20),
        name="stacks",
    )(g, x)


def spread_kernel(rows, pws_ref, rob_ref, w_ref, pws_out, rob_out, w_out, w0, w1, send_sems, lag_sems, ring_sems, last_sems):
    d = lax.axis_index("day")
    l = lax.axis_index("lag")
    z, y = d // 4, lax.rem(d, 4)
    lag_peers = [{"day": d, "lag": lax.rem(l + k, 4)} for k in (1, 2, 3)]
    z_of = [lax.rem(z + k, 4) for k in range(4)]
    y_of = [lax.rem(y + k, 4) for k in range(4)]
    z_peers = [{"day": z_of[k] * 4 + y, "lag": l} for k in (1, 3, 2)]
    y_peers = [{"day": z * 4 + y_of[k], "lag": l} for k in (1, 3, 2)]
    barrier = pltpu.get_barrier_semaphore()
    for peer_id in lag_peers + z_peers + y_peers:
        pl.semaphore_signal(barrier, inc=1, device_id=peer_id)
    pl.semaphore_wait(barrier, 9)

    def push(i, src, dst, sem, to):
        pltpu.make_async_remote_copy(
            src_ref=src, dst_ref=dst, send_sem=send_sems.at[i], recv_sem=sem, device_id=to
        ).start()

    def day_rows(day):
        return pl.ds(pl.multiple_of(day * 4 * rows, 4 * rows), 4 * rows)

    mine = pl.ds(pl.multiple_of((d * 4 + l) * rows, rows), rows)
    srcs, outs = (pws_ref, rob_ref), (pws_out, rob_out)
    for i in range(2):
        for to in lag_peers:
            push(i, srcs[i].at[to["lag"]], outs[i].at[mine], lag_sems.at[i], to)
        pltpu.make_async_copy(srcs[i].at[l], outs[i].at[mine], lag_sems.at[i]).start()
    for to in lag_peers:
        push(2, w_ref, w0.at[l], lag_sems.at[2], to)
    pltpu.make_async_copy(w_ref, w0.at[l], lag_sems.at[2]).start()

    first, second = (z_peers, y_peers), (y_peers, z_peers)
    for i in range(2):
        block = outs[i].at[day_rows(d)]
        pltpu.make_async_copy(block, block, lag_sems.at[i]).wait()
        for n, to in enumerate(first[i]):
            push(i, block, block, ring_sems.at[i, n], to)
        for to in second[i]:
            push(i, block, block, last_sems.at[i], to)
    pltpu.make_async_copy(w0, w0, lag_sems.at[2]).wait()
    for n, k in enumerate((1, 3, 2)):
        push(2, w0.at[:, pl.ds(z_of[k] * 4, 4)], w1.at[z], ring_sems.at[2, n], z_peers[n])
    for n, k in enumerate((1, 3, 2)):
        push(2, w0.at[:, z * 4 + y_of[k]], w_out.at[d], last_sems.at[2], y_peers[n])
    pltpu.make_async_copy(w0.at[:, d], w_out.at[d], last_sems.at[2]).start()
    for n, k in enumerate((3, 1, 2)):
        for i in range(2):
            block = outs[i].at[day_rows((z_of[k] * 4 + y, z * 4 + y_of[k])[i])]
            pltpu.make_async_copy(block, block, ring_sems.at[i, n]).wait()
            for to in second[i]:
                push(i, block, block, last_sems.at[i], to)
        part = w1.at[z_of[k]]
        pltpu.make_async_copy(part, part, ring_sems.at[2, n]).wait()
        for m, j in enumerate((1, 3, 2)):
            push(2, w1.at[z_of[k], :, y_of[j]], w_out.at[z_of[k] * 4 + y], last_sems.at[2], y_peers[m])
        pltpu.make_async_copy(w1.at[z_of[k], :, y], w_out.at[z_of[k] * 4 + y], last_sems.at[2]).start()
    for i in range(2):
        most = outs[i].at[pl.ds(0, 48 * rows)]
        pltpu.make_async_copy(most, most, last_sems.at[i]).wait()
        most = outs[i].at[pl.ds(0, 63 * rows)]
        pltpu.make_async_copy(most, most, send_sems.at[i]).wait()
    pltpu.make_async_copy(w_out, w_out, last_sems.at[2]).wait()
    for part in (w_out, w_out, w_out.at[pl.ds(0, 4)]):
        pltpu.make_async_copy(part, part, send_sems.at[2]).wait()


def spread(pws, rob, w):
    _, rows, width = pws.shape
    out = jax.ShapeDtypeStruct((64 * rows, width), pws.dtype)
    return pl.pallas_call(
        functools.partial(spread_kernel, rows),
        out_shape=(out, out, jax.ShapeDtypeStruct((16, 4, 1, 128), F32)),
        in_specs=[HBM] * 3,
        out_specs=(HBM,) * 3,
        scratch_shapes=[
            pltpu.VMEM((4, 16, 1, 128), F32),
            pltpu.VMEM((4, 4, 4, 1, 128), F32),
            pltpu.SemaphoreType.DMA((3,)),
            pltpu.SemaphoreType.DMA((3,)),
            pltpu.SemaphoreType.DMA((3, 3)),
            pltpu.SemaphoreType.DMA((3,)),
        ],
        compiler_params=pltpu.CompilerParams(collective_id=1, has_side_effects=True),
        name="spread",
    )(pws, rob, w)


def encode(x):
    power = x * x
    power = power * power
    power = power * power
    return jnp.where(x < 0, -power, power).astype(jnp.bfloat16)


def decode(code):
    power = code.astype(F32)
    fourth = lax.rsqrt(lax.rsqrt(jnp.maximum(jnp.abs(power), 2e-38)))
    root = fourth * lax.rsqrt(fourth)
    return jnp.where(power < 0, -root, root)


def per_device(corr):
    pairs, days_here, width = corr.shape
    lags = width * 4
    g = jnp.asarray(hilbert_rows(256, lags))
    pws, rob, w = stacks(g, corr)
    pws = encode(pws[::4].reshape(16, 4, width).transpose(1, 0, 2))
    rob = encode(rob[::4].reshape(16, 4, width).transpose(1, 0, 2))
    pws, rob, w = spread(pws, rob, w)
    w = w.reshape(64, 128)
    pws = decode(pws).reshape(64, 16, width) * w[:, 64].reshape(64, 1, 1)
    rob = decode(rob).reshape(64, 16, width) * w[:, 65].reshape(64, 1, 1)
    return pws.reshape(pairs, width), rob.reshape(pairs, width), w[:, :64].reshape(pairs, days_here)


def solution(mesh):
    return jax.shard_map(
        per_device,
        mesh=mesh,
        in_specs=(P("pair", "day", "lag"),),
        out_specs=(P("pair", "lag"), P("pair", "lag"), P("pair", "day")),
        check_vma=False,
    )
```

```python
import functools

import jax
import jax.numpy as jnp
import numpy as np
from jax import lax
from jax.experimental import pallas as pl
from jax.experimental.pallas import tpu as pltpu
from jax.sharding import PartitionSpec as P

ITERS = 3
EPS = 1e-06
HBM = pl.BlockSpec(memory_space=pl.ANY)
VMEM = pl.BlockSpec(memory_space=pltpu.VMEM)
F32 = jnp.float32


def hilbert_rows(rows, lags):
    offset = (np.arange(lags)[None, :] - np.arange(rows)[:, None]) % lags
    odd = offset % 2 == 1
    angle = np.pi * offset / lags
    value = np.where(odd, 2.0 / lags * np.cos(angle) / np.where(odd, np.sin(angle), 1.0), 0.0)
    return value.astype(np.float32).astype(jnp.bfloat16)


def peer(k, me_d, me_l):
    a = lax.rem(k, 4)
    z = lax.rem(me_d // 4 + a + k // 4, 4)
    y = lax.rem(lax.rem(me_d, 4) + a, 4)
    x = lax.rem(me_l // 2 + a + k // 16, 2)
    c = lax.rem(me_l + k // 32, 2)
    return z * 4 + y, x * 2 + c


def entry_barrier(d, l):
    barrier = pltpu.get_barrier_semaphore()

    def greet(k, carry):
        td, tl = peer(k, d, l)
        pl.semaphore_signal(barrier, inc=1, device_id={"day": td, "lag": tl})
        return carry

    lax.fori_loop(1, 64, greet, 0)
    pl.semaphore_wait(barrier, 63)


def group4(x):
    n = x.shape[0]
    row = lax.broadcasted_iota(jnp.int32, x.shape, 0)
    other = jnp.where(row % 2 == 0, pltpu.roll(x, n - 1, 0), pltpu.roll(x, 1, 0))
    x = x + other
    other = jnp.where(row % 4 < 2, pltpu.roll(x, n - 2, 0), pltpu.roll(x, 2, 0))
    return x + other


def wide(x, lanes):
    return jnp.concatenate([x] * (lanes // 128), axis=1)


def fold(x):
    total = x[:, :128]
    for j in range(128, x.shape[1], 128):
        total = total + x[:, j:j + 128]
    return total


def lane_sum(ref):
    ndev, rows, lanes = ref.shape
    total = jnp.sum(ref[...].reshape(ndev * rows, lanes), axis=1, keepdims=True)
    return jnp.broadcast_to(total, (ndev * rows, lanes)).reshape(ndev, rows, lanes)


def day_sum(x):
    total = x[0]
    for d in range(1, x.shape[0]):
        total = total + x[d]
    return group4(total)


def stack_kernel(parts, g_ref, x_ref, pws_ref, rob_ref, w_ref,
                 recv, k_ref, xb_ref, x32_ref, st_ref, part_ref, inv_ref, coh_ref, wt_ref, share_ref,
                 send_sem, recv_sems):
    me_d = lax.axis_index("day")
    me_l = lax.axis_index("lag")
    ndev, quads, here, lags = recv.shape[1:]
    rows = quads * here
    days = ndev * here
    width = lags // 4
    entry_barrier(me_d, me_l)
    lanes = pl.ds(pl.multiple_of(me_l * width, width), width)

    def block(r, td, tl):
        return x_ref.at[pl.ds(((td * 4 + tl) * parts + r) * quads, quads)]

    for r in range(parts):
        def send(k, carry):
            td, tl = peer(k, me_d, me_l)
            pltpu.make_async_remote_copy(
                src_ref=block(r, td, tl),
                dst_ref=recv.at[r, me_d, :, :, lanes],
                send_sem=send_sem,
                recv_sem=recv_sems.at[r],
                device_id={"day": td, "lag": tl},
            ).start()
            return carry

        lax.fori_loop(1, 64, send, 0)
        pltpu.make_async_copy(block(r, me_d, me_l), recv.at[r, me_d, :, :, lanes], recv_sems.at[r]).start()

    step = g_ref.shape[0]
    for i in range(lags // step):
        cut = i * step
        if cut:
            k_ref[cut:cut + step, :cut] = g_ref[:, lags - cut:]
        k_ref[cut:cut + step, cut:] = g_ref[:, :lags - cut]

    def one_part(r, carry):
        pltpu.make_async_copy(recv.at[r], recv.at[r], recv_sems.at[r]).wait()

        @pl.loop(0, ndev, unroll=2)
        def _(d):
            x = recv[r, d].reshape(rows, lags)
            xb_ref[d] = x
            data = x.astype(F32)
            x32_ref[d] = data
            part_ref[d] = fold(data * data)

        inv_ref[...] = 1.0 / jnp.sqrt(lane_sum(part_ref) / lags + EPS)
        tile = 256

        @pl.loop(0, lags // tile, unroll=2)
        def _(t):
            at = pl.ds(pl.multiple_of(t * tile, tile), tile)
            quad = jnp.dot(xb_ref[...].reshape(ndev * rows, lags), k_ref[:, at], preferred_element_type=F32)
            lin = jnp.zeros((rows, tile), F32)
            csum = jnp.zeros((rows, tile), F32)
            ssum = jnp.zeros((rows, tile), F32)
            for d in range(ndev):
                data = x32_ref[d, :, at]
                q = quad[d * rows:(d + 1) * rows]
                scale = wide(inv_ref[d], tile)
                inv = jnp.minimum(lax.rsqrt(data * data + q * q), 10.0 * scale)
                lin = lin + data * scale
                csum = csum + data * inv
                ssum = ssum + q * inv
            csum = group4(csum)
            ssum = group4(ssum)
            st_ref[:, at] = group4(lin) / days * ((csum * csum + ssum * ssum) / (days * days))

        out = pl.ds(pl.multiple_of(r * rows, rows), rows)
        pws_ref[out, :] = st_ref[...]
        for step in range(ITERS):
            stack = st_ref[...]
            msq = jnp.sum(fold(stack * stack), axis=1, keepdims=True) / lags
            st_ref[...] = stack * (1.0 / jnp.sqrt(msq + EPS))

            @pl.loop(0, ndev, unroll=4)
            def _(d):
                part_ref[d] = fold(x32_ref[d] * st_ref[...])

            coh_ref[...] = lane_sum(part_ref) * inv_ref[...] / lags

            @pl.loop(0, ndev, unroll=4)
            def _(d):
                diff = x32_ref[d] * wide(inv_ref[d], lags) - wide(coh_ref[d], lags) * st_ref[...]
                part_ref[d] = fold(diff * diff)

            res = lane_sum(part_ref) / lags
            rbar = day_sum(res) / days
            weight = (0.1 + jnp.abs(coh_ref[...])) / (res + rbar + EPS)
            total = day_sum(weight)
            wt_ref[...] = weight * inv_ref[...]
            chunk = 512

            @pl.loop(0, lags // chunk)
            def _(t):
                at = pl.ds(pl.multiple_of(t * chunk, chunk), chunk)
                mix = wide(wt_ref[0], chunk) * x32_ref[0, :, at]
                for d in range(1, ndev):
                    mix = mix + wide(wt_ref[d], chunk) * x32_ref[d, :, at]
                st_ref[:, at] = group4(mix)

            if step == ITERS - 1:
                rob_ref[out, :] = st_ref[...] * wide(1.0 / total, lags)
                lane = lax.broadcasted_iota(jnp.int32, (rows, 128), 1)
                shares = jnp.zeros((rows, 128), F32)
                for d in range(ndev):
                    shares = jnp.where(lane == d, weight[d] / total, shares)
                share_ref[out, :] = shares
        return carry

    lax.fori_loop(0, parts, one_part, 0)
    units = []
    for ref in (pws_ref, rob_ref):
        top = jnp.max(jnp.abs(ref[...]), axis=(0, 1), keepdims=True)
        top = jnp.maximum(top, 1e-30)
        ref[...] = ref[...] * (16384.0 / top)
        units.append(jnp.broadcast_to(top / 16384.0, (1, 128)))
    shares = share_ref[...].T
    lane = lax.broadcasted_iota(jnp.int32, (1, 128), 1)
    for d in range(ndev):
        row = jnp.where(lane == 64, units[0], shares[d:d + 1])
        w_ref[d] = jnp.where(lane == 65, units[1], row)
    for r in range(parts):
        most = x_ref.at[pl.ds(0, 63 * quads)]
        pltpu.make_async_copy(most, most, send_sem).wait()


def stacks(g, x):
    pairs, here, width = x.shape
    lags = 4 * width
    parts = 4
    quads = pairs // 64 // parts
    rows = pairs // 64 * here
    part = quads * here
    out = jax.ShapeDtypeStruct((rows, lags), F32)
    thin = pltpu.VMEM((16, part, 128), F32)
    return pl.pallas_call(
        functools.partial(stack_kernel, parts),
        out_shape=(out, out, jax.ShapeDtypeStruct((16, 1, 128), F32)),
        in_specs=[VMEM, HBM],
        out_specs=(VMEM,) * 3,
        scratch_shapes=[
            pltpu.VMEM((parts, 16, quads, here, lags), x.dtype),
            pltpu.VMEM((lags, lags), jnp.bfloat16),
            pltpu.VMEM((16, part, lags), jnp.bfloat16),
            pltpu.VMEM((16, part, lags), F32),
            pltpu.VMEM((part, lags), F32),
            thin, thin, thin, thin,
            pltpu.VMEM((128, 128), F32),
            pltpu.SemaphoreType.DMA,
            pltpu.SemaphoreType.DMA((parts,)),
        ],
        compiler_params=pltpu.CompilerParams(collective_id=0, has_side_effects=True, vmem_limit_bytes=50 * 2**20),
        name="stacks",
    )(g, x)


def spread_kernel(rows, pws_ref, rob_ref, w_ref, pws_out, rob_out, w_out, w0, w1, send_sems, lag_sems, ring_sems, last_sems):
    d = lax.axis_index("day")
    l = lax.axis_index("lag")
    z, y = d // 4, lax.rem(d, 4)
    lag_peers = [{"day": d, "lag": lax.rem(l + k, 4)} for k in (1, 2, 3)]
    z_of = [lax.rem(z + k, 4) for k in range(4)]
    y_of = [lax.rem(y + k, 4) for k in range(4)]
    z_peers = [{"day": z_of[k] * 4 + y, "lag": l} for k in (1, 3, 2)]
    y_peers = [{"day": z * 4 + y_of[k], "lag": l} for k in (1, 3, 2)]
    barrier = pltpu.get_barrier_semaphore()
    for peer_id in lag_peers + z_peers + y_peers:
        pl.semaphore_signal(barrier, inc=1, device_id=peer_id)
    pl.semaphore_wait(barrier, 9)

    def push(i, src, dst, sem, to):
        pltpu.make_async_remote_copy(
            src_ref=src, dst_ref=dst, send_sem=send_sems.at[i], recv_sem=sem, device_id=to
        ).start()

    def day_rows(day):
        return pl.ds(pl.multiple_of(day * 4 * rows, 4 * rows), 4 * rows)

    mine = pl.ds(pl.multiple_of((d * 4 + l) * rows, rows), rows)
    srcs, outs = (pws_ref, rob_ref), (pws_out, rob_out)
    for i in range(2):
        for to in lag_peers:
            push(i, srcs[i].at[to["lag"]], outs[i].at[mine], lag_sems.at[i], to)
        pltpu.make_async_copy(srcs[i].at[l], outs[i].at[mine], lag_sems.at[i]).start()
    for to in lag_peers:
        push(2, w_ref, w0.at[l], lag_sems.at[2], to)
    pltpu.make_async_copy(w_ref, w0.at[l], lag_sems.at[2]).start()

    first, second = (z_peers, y_peers), (y_peers, z_peers)
    for i in range(2):
        block = outs[i].at[day_rows(d)]
        pltpu.make_async_copy(block, block, lag_sems.at[i]).wait()
        for n, to in enumerate(first[i]):
            push(i, block, block, ring_sems.at[i, n], to)
        for to in second[i]:
            push(i, block, block, last_sems.at[i], to)
    pltpu.make_async_copy(w0, w0, lag_sems.at[2]).wait()
    for n, k in enumerate((1, 3, 2)):
        push(2, w0.at[:, pl.ds(z_of[k] * 4, 4)], w1.at[z], ring_sems.at[2, n], z_peers[n])
    for n, k in enumerate((1, 3, 2)):
        push(2, w0.at[:, z * 4 + y_of[k]], w_out.at[d], last_sems.at[2], y_peers[n])
    pltpu.make_async_copy(w0.at[:, d], w_out.at[d], last_sems.at[2]).start()
    for n, k in enumerate((3, 1, 2)):
        for i in range(2):
            block = outs[i].at[day_rows((z_of[k] * 4 + y, z * 4 + y_of[k])[i])]
            pltpu.make_async_copy(block, block, ring_sems.at[i, n]).wait()
            for to in second[i]:
                push(i, block, block, last_sems.at[i], to)
        part = w1.at[z_of[k]]
        pltpu.make_async_copy(part, part, ring_sems.at[2, n]).wait()
        for m, j in enumerate((1, 3, 2)):
            push(2, w1.at[z_of[k], :, y_of[j]], w_out.at[z_of[k] * 4 + y], last_sems.at[2], y_peers[m])
        pltpu.make_async_copy(w1.at[z_of[k], :, y], w_out.at[z_of[k] * 4 + y], last_sems.at[2]).start()
    for i in range(2):
        most = outs[i].at[pl.ds(0, 48 * rows)]
        pltpu.make_async_copy(most, most, last_sems.at[i]).wait()
        most = outs[i].at[pl.ds(0, 63 * rows)]
        pltpu.make_async_copy(most, most, send_sems.at[i]).wait()
    pltpu.make_async_copy(w_out, w_out, last_sems.at[2]).wait()
    for part in (w_out, w_out, w_out.at[pl.ds(0, 4)]):
        pltpu.make_async_copy(part, part, send_sems.at[2]).wait()


def spread(pws, rob, w):
    _, rows, width = pws.shape
    out = jax.ShapeDtypeStruct((64 * rows, width), pws.dtype)
    return pl.pallas_call(
        functools.partial(spread_kernel, rows),
        out_shape=(out, out, jax.ShapeDtypeStruct((16, 4, 1, 128), F32)),
        in_specs=[HBM] * 3,
        out_specs=(HBM,) * 3,
        scratch_shapes=[
            pltpu.VMEM((4, 16, 1, 128), F32),
            pltpu.VMEM((4, 4, 4, 1, 128), F32),
            pltpu.SemaphoreType.DMA((3,)),
            pltpu.SemaphoreType.DMA((3,)),
            pltpu.SemaphoreType.DMA((3, 3)),
            pltpu.SemaphoreType.DMA((3,)),
        ],
        compiler_params=pltpu.CompilerParams(collective_id=1, has_side_effects=True),
        name="spread",
    )(pws, rob, w)


def encode(x):
    power = x * x
    power = power * power
    power = power * power
    return jnp.where(x < 0, -power, power).astype(jnp.bfloat16)


def decode(code):
    power = code.astype(F32)
    fourth = lax.rsqrt(lax.rsqrt(jnp.maximum(jnp.abs(power), 2e-38)))
    root = fourth * lax.rsqrt(fourth)
    return jnp.where(power < 0, -root, root)


def per_device(corr):
    pairs, days_here, width = corr.shape
    lags = width * 4
    g = jnp.asarray(hilbert_rows(256, lags))
    pws, rob, w = stacks(g, corr)
    pws = encode(pws[::4].reshape(16, 4, width).transpose(1, 0, 2))
    rob = encode(rob[::4].reshape(16, 4, width).transpose(1, 0, 2))
    pws, rob, w = spread(pws, rob, w)
    w = w.reshape(64, 128)
    pws = decode(pws).reshape(64, 16, width) * w[:, 64].reshape(64, 1, 1)
    rob = decode(rob).reshape(64, 16, width) * w[:, 65].reshape(64, 1, 1)
    return pws.reshape(pairs, width), rob.reshape(pairs, width), w[:, :64].reshape(pairs, days_here)


def solution(mesh):
    return jax.shard_map(
        per_device,
        mesh=mesh,
        in_specs=(P("pair", "day", "lag"),),
        out_specs=(P("pair", "lag"), P("pair", "lag"), P("pair", "day")),
        check_vma=False,
    )
```

```python
import functools

import jax
import jax.numpy as jnp
import numpy as np
from jax import lax
from jax.experimental import pallas as pl
from jax.experimental.pallas import tpu as pltpu
from jax.sharding import PartitionSpec as P

ITERS = 3
EPS = 1e-06
HBM = pl.BlockSpec(memory_space=pl.ANY)
VMEM = pl.BlockSpec(memory_space=pltpu.VMEM)
F32 = jnp.float32


def hilbert_rows(rows, lags):
    offset = (np.arange(lags)[None, :] - np.arange(rows)[:, None]) % lags
    odd = offset % 2 == 1
    angle = np.pi * offset / lags
    value = np.where(odd, 2.0 / lags * np.cos(angle) / np.where(odd, np.sin(angle), 1.0), 0.0)
    return value.astype(np.float32).astype(jnp.bfloat16)


def peer(k, me_d, me_l):
    a = lax.rem(k, 4)
    z = lax.rem(me_d // 4 + a + k // 4, 4)
    y = lax.rem(lax.rem(me_d, 4) + a, 4)
    x = lax.rem(me_l // 2 + a + k // 16, 2)
    c = lax.rem(me_l + k // 32, 2)
    return z * 4 + y, x * 2 + c


def entry_barrier(d, l):
    barrier = pltpu.get_barrier_semaphore()

    def greet(k, carry):
        td, tl = peer(k, d, l)
        pl.semaphore_signal(barrier, inc=1, device_id={"day": td, "lag": tl})
        return carry

    lax.fori_loop(1, 64, greet, 0)
    pl.semaphore_wait(barrier, 63)


def group4(x):
    n = x.shape[0]
    row = lax.broadcasted_iota(jnp.int32, x.shape, 0)
    other = jnp.where(row % 2 == 0, pltpu.roll(x, n - 1, 0), pltpu.roll(x, 1, 0))
    x = x + other
    other = jnp.where(row % 4 < 2, pltpu.roll(x, n - 2, 0), pltpu.roll(x, 2, 0))
    return x + other


def wide(x, lanes):
    return jnp.concatenate([x] * (lanes // 128), axis=1)


def fold(x):
    total = x[:, :128]
    for j in range(128, x.shape[1], 128):
        total = total + x[:, j:j + 128]
    return total


def lane_sum(ref):
    ndev, rows, lanes = ref.shape
    total = jnp.sum(ref[...].reshape(ndev * rows, lanes), axis=1, keepdims=True)
    return jnp.broadcast_to(total, (ndev * rows, lanes)).reshape(ndev, rows, lanes)


def day_sum(x):
    total = x[0]
    for d in range(1, x.shape[0]):
        total = total + x[d]
    return group4(total)


def encode(x):
    power = x * x
    power = power * power
    power = power * power
    return jnp.where(x < 0, -power, power).astype(jnp.bfloat16)


def decode(code):
    power = code.astype(F32)
    fourth = lax.rsqrt(lax.rsqrt(jnp.maximum(jnp.abs(power), 2e-38)))
    root = fourth * lax.rsqrt(fourth)
    return jnp.where(power < 0, -root, root)


def stack_kernel(parts, g_ref, x_ref, pws_out, rob_out, tail_out,
                 recv, gv_ref, k_ref, xb_ref, x32_ref, st_ref, part_ref, inv_ref, coh_ref, wt_ref, share_ref, unit_ref,
                 pws_code, rob_code, tail_code,
                 g_sem, send_sem, recv_sems, out_sems, lag_sems, ring_sems, last_sems, tail_sems):
    me_d = lax.axis_index("day")
    me_l = lax.axis_index("lag")
    ndev, quads, here, lags = recv.shape[1:]
    rows = quads * here
    days = ndev * here
    width = lags // 4
    early = parts - 1
    fetch = pltpu.make_async_copy(g_ref, gv_ref, g_sem)
    fetch.start()
    entry_barrier(me_d, me_l)
    lanes = pl.ds(pl.multiple_of(me_l * width, width), width)

    def block(r, td, tl):
        return x_ref.at[pl.ds(((td * 4 + tl) * parts + r) * quads, quads)]

    for r in range(parts):
        def send(k, carry):
            td, tl = peer(k, me_d, me_l)
            pltpu.make_async_remote_copy(
                src_ref=block(r, td, tl),
                dst_ref=recv.at[r, me_d, :, :, lanes],
                send_sem=send_sem,
                recv_sem=recv_sems.at[r],
                device_id={"day": td, "lag": tl},
            ).start()
            return carry

        lax.fori_loop(1, 64, send, 0)
        pltpu.make_async_copy(block(r, me_d, me_l), recv.at[r, me_d, :, :, lanes], recv_sems.at[r]).start()

    fetch.wait()
    step = g_ref.shape[0]
    for i in range(lags // step):
        cut = i * step
        if cut:
            k_ref[cut:cut + step, :cut] = gv_ref[:, lags - cut:]
        k_ref[cut:cut + step, cut:] = gv_ref[:, :lags - cut]

    z, y = me_d // 4, lax.rem(me_d, 4)
    z_of = [lax.rem(z + k, 4) for k in range(4)]
    y_of = [lax.rem(y + k, 4) for k in range(4)]
    lag_peers = [lax.rem(me_l + k, 4) for k in (1, 2, 3)]
    z_peers = [{"day": z_of[k] * 4 + y, "lag": me_l} for k in (1, 3, 2)]
    y_peers = [{"day": z * 4 + y_of[k], "lag": me_l} for k in (1, 3, 2)]
    first, second = (z_peers, y_peers, z_peers), (y_peers, z_peers, y_peers)
    codes, outs = (pws_code, rob_code, pws_code), (pws_out, rob_out, pws_out)
    spans = (pl.ds(0, early), pl.ds(0, early), pl.ds(early, 1))

    def push(i, src, dst, sem, to):
        pltpu.make_async_remote_copy(
            src_ref=src, dst_ref=dst, send_sem=out_sems.at[i], recv_sem=sem, device_id=to
        ).start()

    def to_lag_group(i):
        dst = outs[i].at[spans[i], me_d, me_l]
        for tl in lag_peers:
            push(i, codes[i].at[spans[i], tl], dst, lag_sems.at[i], {"day": me_d, "lag": tl})
        pltpu.make_async_copy(codes[i].at[spans[i], me_l], dst, lag_sems.at[i]).start()

    def to_rings(i):
        own = outs[i].at[spans[i], me_d]
        pltpu.make_async_copy(own, own, lag_sems.at[i]).wait()
        for n, to in enumerate(first[i]):
            push(i, own, own, ring_sems.at[i, n], to)
        for to in second[i]:
            push(i, own, own, last_sems.at[i], to)

    def forward(i):
        for n, k in enumerate((3, 1, 2)):
            day = (z_of[k] * 4 + y, z * 4 + y_of[k], z_of[k] * 4 + y)[i]
            got = outs[i].at[spans[i], day]
            pltpu.make_async_copy(got, got, ring_sems.at[i, n]).wait()
            for to in second[i]:
                push(i, got, got, last_sems.at[i], to)

    def finish(i):
        most = outs[i].at[spans[i], pl.ds(0, 12)]
        pltpu.make_async_copy(most, most, last_sems.at[i]).wait()
        for part in (outs[i].at[spans[i], pl.ds(0, 15)], codes[i].at[spans[i], pl.ds(0, 3)]):
            pltpu.make_async_copy(part, part, out_sems.at[i]).wait()

    def coded(slot):
        top = jnp.max(jnp.abs(st_ref[...]), axis=(0, 1), keepdims=True)
        top = jnp.maximum(top, 1e-30)
        unit_ref[slot] = jnp.broadcast_to(top / 16384.0, (1, 128))
        stack = st_ref[...]
        stack = jnp.concatenate([stack[j * here:j * here + 1] for j in range(quads)], axis=0)
        return encode(stack * (16384.0 / top))

    def one_part(r, hooks):
        hooks[0]()
        pltpu.make_async_copy(recv.at[r], recv.at[r], recv_sems.at[r]).wait()

        @pl.loop(0, ndev, unroll=2)
        def _(d):
            x = recv[r, d].reshape(rows, lags)
            xb_ref[d] = x
            data = x.astype(F32)
            x32_ref[d] = data
            part_ref[d] = fold(data * data)

        inv_ref[...] = 1.0 / jnp.sqrt(lane_sum(part_ref) / lags + EPS)
        hooks[1]()
        tile = 256

        @pl.loop(0, lags // tile, unroll=2)
        def _(t):
            at = pl.ds(pl.multiple_of(t * tile, tile), tile)
            quad = jnp.dot(xb_ref[...].reshape(ndev * rows, lags), k_ref[:, at], preferred_element_type=F32)
            lin = jnp.zeros((rows, tile), F32)
            csum = jnp.zeros((rows, tile), F32)
            ssum = jnp.zeros((rows, tile), F32)
            for d in range(ndev):
                data = x32_ref[d, :, at]
                q = quad[d * rows:(d + 1) * rows]
                scale = wide(inv_ref[d], tile)
                inv = jnp.minimum(lax.rsqrt(data * data + q * q), 10.0 * scale)
                lin = lin + data * scale
                csum = csum + data * inv
                ssum = ssum + q * inv
            csum = group4(csum)
            ssum = group4(ssum)
            st_ref[:, at] = group4(lin) / days * ((csum * csum + ssum * ssum) / (days * days))

        code = coded(r)
        for j in range(4):
            pws_code[r, j] = code[:, j * width:(j + 1) * width]
        hooks[2]()
        for step in range(ITERS):
            stack = st_ref[...]
            msq = jnp.sum(fold(stack * stack), axis=1, keepdims=True) / lags
            st_ref[...] = stack * (1.0 / jnp.sqrt(msq + EPS))

            @pl.loop(0, ndev, unroll=4)
            def _(d):
                part_ref[d] = fold(x32_ref[d] * st_ref[...])

            coh_ref[...] = lane_sum(part_ref) * inv_ref[...] / lags

            @pl.loop(0, ndev, unroll=4)
            def _(d):
                diff = x32_ref[d] * wide(inv_ref[d], lags) - wide(coh_ref[d], lags) * st_ref[...]
                part_ref[d] = fold(diff * diff)

            res = lane_sum(part_ref) / lags
            rbar = day_sum(res) / days
            weight = (0.1 + jnp.abs(coh_ref[...])) / (res + rbar + EPS)
            total = day_sum(weight)
            wt_ref[...] = weight * inv_ref[...]
            chunk = 512

            @pl.loop(0, lags // chunk)
            def _(t):
                at = pl.ds(pl.multiple_of(t * chunk, chunk), chunk)
                mix = wide(wt_ref[0], chunk) * x32_ref[0, :, at]
                for d in range(1, ndev):
                    mix = mix + wide(wt_ref[d], chunk) * x32_ref[d, :, at]
                st_ref[:, at] = group4(mix)

            if step < ITERS - 1:
                hooks[3 + step]()
        st_ref[...] = st_ref[...] * wide(1.0 / total, lags)
        lane = lax.broadcasted_iota(jnp.int32, (rows, 128), 1)
        shares = jnp.zeros((rows, 128), F32)
        for d in range(ndev):
            shares = jnp.where(lane == d, weight[d] / total, shares)
        share_ref[pl.ds(pl.multiple_of(r * rows, rows), rows), :] = shares
        return coded(parts + r)

    def early_part(r, carry):
        code = one_part(r, [lambda: None] * 5)
        for j in range(4):
            rob_code[r, j] = code[:, j * width:(j + 1) * width]
        return carry

    lax.fori_loop(0, early, early_part, 0)

    def each(action, *items):
        return lambda: [action(i) for i in items]

    def after_phase():
        forward(0)
        forward(1)
        to_lag_group(2)

    code = one_part(early, [each(to_lag_group, 0, 1), each(to_rings, 0, 1), after_phase, each(to_rings, 2), each(forward, 2)])

    lane = lax.broadcasted_iota(jnp.int32, (1, 128), 1)
    extra = jnp.zeros((1, 128), F32)
    for j in range(2 * parts):
        extra = jnp.where(lane == 64 + j, unit_ref[j], extra)
    row = lax.broadcasted_iota(jnp.int32, (here, 128), 0)
    words = share_ref[...].T[:ndev]
    words = jnp.where(lax.broadcasted_iota(jnp.int32, words.shape, 1) < 64, words, extra)
    high = words.astype(jnp.bfloat16).astype(F32)
    mid = (words - high).astype(jnp.bfloat16).astype(F32)
    low = words - high - mid
    for d in range(ndev):
        piece = jnp.where(row == 0, high[d:d + 1], jnp.where(row == 1, mid[d:d + 1], low[d:d + 1])).astype(jnp.bfloat16)
        for j in range(4):
            tail_code[d, j, :, :width] = code[:, j * width:(j + 1) * width]
            tail_code[d, j, :, width:] = piece

    def send_tail(k, carry):
        td, tl = peer(k, me_d, me_l)
        pltpu.make_async_remote_copy(
            src_ref=tail_code.at[td, tl], dst_ref=tail_out.at[me_d, me_l],
            send_sem=tail_sems.at[0], recv_sem=tail_sems.at[1], device_id={"day": td, "lag": tl},
        ).start()
        return carry

    lax.fori_loop(1, 64, send_tail, 0)
    pltpu.make_async_copy(tail_code.at[me_d, me_l], tail_out.at[me_d, me_l], tail_sems.at[1]).start()
    for r in range(parts):
        most = x_ref.at[pl.ds(0, 63 * quads)]
        pltpu.make_async_copy(most, most, send_sem).wait()
    for i in range(3):
        finish(i)
    pltpu.make_async_copy(tail_out, tail_out, tail_sems.at[1]).wait()
    for part in (tail_code.at[pl.ds(0, ndev - 1)], tail_code.at[ndev - 1, pl.ds(0, 3)]):
        pltpu.make_async_copy(part, part, tail_sems.at[0]).wait()


def stacks(g, x):
    pairs, here, width = x.shape
    lags = 4 * width
    parts = 4
    quads = pairs // 64 // parts
    part = quads * here
    thin = pltpu.VMEM((16, part, 128), F32)
    dma = pltpu.SemaphoreType.DMA
    bf16 = jnp.bfloat16
    return pl.pallas_call(
        functools.partial(stack_kernel, parts),
        out_shape=(
            jax.ShapeDtypeStruct((parts, 16, 4, quads, width), bf16),
            jax.ShapeDtypeStruct((parts - 1, 16, 4, quads, width), bf16),
            jax.ShapeDtypeStruct((16, 4, quads, width + 128), bf16),
        ),
        in_specs=[HBM, HBM],
        out_specs=(HBM,) * 3,
        scratch_shapes=[
            pltpu.VMEM((parts, 16, quads, here, lags), x.dtype),
            pltpu.VMEM(g.shape, bf16),
            pltpu.VMEM((lags, lags), bf16),
            pltpu.VMEM((16, part, lags), bf16),
            pltpu.VMEM((16, part, lags), F32),
            pltpu.VMEM((part, lags), F32),
            thin, thin, thin, thin,
            pltpu.VMEM((128, 128), F32),
            pltpu.VMEM((2 * parts, 1, 128), F32),
            pltpu.VMEM((parts, 4, quads, width), bf16),
            pltpu.VMEM((parts - 1, 4, quads, width), bf16),
            pltpu.VMEM((16, 4, quads, width + 128), bf16),
            dma, dma, dma((parts,)), dma((3,)), dma((3,)), dma((3, 3)), dma((3,)), dma((2,)),
        ],
        compiler_params=pltpu.CompilerParams(collective_id=0, has_side_effects=True, vmem_limit_bytes=63 * 2**20),
        name="stacks",
    )(g, x)


def decode_kernel(pws_ref, rob_ref, tail_ref, pws_out, rob_out, w_out, words_ref):
    step = pl.program_id(0)
    parts, here, _, quads, width = pws_ref.shape
    count = parts * quads
    lane = lax.broadcasted_iota(jnp.int32, (count, 128), 1)
    slot = lax.broadcasted_iota(jnp.int32, (count, 128), 0) // quads + 64
    for d in range(here):
        for l in range(4):
            c = d * 4 + l
            word = jnp.sum(tail_ref[d, l, :, width:].astype(F32)[:3], axis=0, keepdims=True)
            words_ref[step * here * 4 + c] = word
            units = []
            for base in (0, parts):
                units.append(jnp.sum(jnp.where(lane == slot + base, word, 0.0), axis=1, keepdims=True))
            at = slice(c * count, (c + 1) * count)
            pws_out[at, :] = decode(pws_ref[:, d, l].reshape(count, width)) * units[0]
            rob = [rob_ref[r, d, l].astype(F32) for r in range(parts - 1)] + [tail_ref[d, l, :, :width].astype(F32)]
            rob_out[at, :] = decode(jnp.concatenate(rob, axis=0)) * units[1]

    @pl.when(step == pl.num_programs(0) - 1)
    def _():
        words = words_ref[...].reshape(64, 128)
        source = lax.broadcasted_iota(jnp.int32, (128, 128), 0)
        target = lax.broadcasted_iota(jnp.int32, (128, 128), 1)
        row = lax.broadcasted_iota(jnp.int32, (64, 128), 0)
        mine = lax.broadcasted_iota(jnp.int32, (64, 128), 1) // 16 == row % 8
        for dd in range(w_out.shape[0]):
            pick = jnp.where(source == target % 16 * 4 + dd, 1.0, 0.0)
            moved = jnp.dot(words, pick, precision=lax.Precision.HIGHEST, preferred_element_type=F32)
            moved = jnp.where(mine, moved, 0.0)
            for j in range(8):
                w_out[dd:dd + 1, j * 128:(j + 1) * 128] = jnp.sum(moved[j * 8:j * 8 + 8], axis=0, keepdims=True)


def decoded(pws, rob, tail):
    parts, days, _, quads, width = pws.shape
    here = 4
    pairs = 64 * parts * quads
    count = pairs * here // days
    big = jax.ShapeDtypeStruct((pairs, width), F32)
    row = pl.BlockSpec((count, width), lambda i: (i, 0))
    return pl.pallas_call(
        decode_kernel,
        out_shape=(big, big, jax.ShapeDtypeStruct((4, pairs), F32)),
        grid=(days // here,),
        in_specs=[
            pl.BlockSpec((parts, here, 4, quads, width), lambda i: (0, i, 0, 0, 0)),
            pl.BlockSpec((parts - 1, here, 4, quads, width), lambda i: (0, i, 0, 0, 0)),
            pl.BlockSpec((here, 4, quads, width + 128), lambda i: (i, 0, 0, 0)),
        ],
        out_specs=(row, row, pl.BlockSpec((4, pairs), lambda i: (0, 0))),
        scratch_shapes=[pltpu.VMEM((64, 1, 128), F32)],
        compiler_params=pltpu.CompilerParams(vmem_limit_bytes=63 * 2**20),
        name="decoded",
    )(pws, rob, tail)


def per_device(corr):
    g = jnp.asarray(hilbert_rows(256, corr.shape[2] * 4))
    pws, rob, shares = decoded(*stacks(g, corr))
    return pws, rob, shares.T


def solution(mesh):
    return jax.shard_map(
        per_device,
        mesh=mesh,
        in_specs=(P("pair", "day", "lag"),),
        out_specs=(P("pair", "lag"), P("pair", "lag"), P("pair", "day")),
        check_vma=False,
    )
```

```python
import functools

import jax
import jax.numpy as jnp
import numpy as np
from jax import lax
from jax.experimental import pallas as pl
from jax.experimental.pallas import tpu as pltpu
from jax.sharding import PartitionSpec as P

ITERS = 3
EPS = 1e-06
HBM = pl.BlockSpec(memory_space=pl.ANY)
VMEM = pl.BlockSpec(memory_space=pltpu.VMEM)
F32 = jnp.float32


def hilbert_rows(rows, lags):
    offset = (np.arange(lags)[None, :] - np.arange(rows)[:, None]) % lags
    odd = offset % 2 == 1
    angle = np.pi * offset / lags
    value = np.where(odd, 2.0 / lags * np.cos(angle) / np.where(odd, np.sin(angle), 1.0), 0.0)
    return value.astype(np.float32).astype(jnp.bfloat16)


def peer(k, me_d, me_l):
    a = lax.rem(k, 4)
    z = lax.rem(me_d // 4 + a + k // 4, 4)
    y = lax.rem(lax.rem(me_d, 4) + a, 4)
    x = lax.rem(me_l // 2 + a + k // 16, 2)
    c = lax.rem(me_l + k // 32, 2)
    return z * 4 + y, x * 2 + c


def entry_barrier(d, l):
    barrier = pltpu.get_barrier_semaphore()

    def greet(k, carry):
        td, tl = peer(k, d, l)
        pl.semaphore_signal(barrier, inc=1, device_id={"day": td, "lag": tl})
        return carry

    lax.fori_loop(1, 64, greet, 0)
    pl.semaphore_wait(barrier, 63)


def group4(x):
    n = x.shape[0]
    row = lax.broadcasted_iota(jnp.int32, x.shape, 0)
    other = jnp.where(row % 2 == 0, pltpu.roll(x, n - 1, 0), pltpu.roll(x, 1, 0))
    x = x + other
    other = jnp.where(row % 4 < 2, pltpu.roll(x, n - 2, 0), pltpu.roll(x, 2, 0))
    return x + other


def wide(x, lanes):
    return jnp.concatenate([x] * (lanes // 128), axis=1)


def fold(x):
    total = x[:, :128]
    for j in range(128, x.shape[1], 128):
        total = total + x[:, j:j + 128]
    return total


def lane_sum(ref):
    ndev, rows, lanes = ref.shape
    total = jnp.sum(ref[...].reshape(ndev * rows, lanes), axis=1, keepdims=True)
    return jnp.broadcast_to(total, (ndev * rows, lanes)).reshape(ndev, rows, lanes)


def day_sum(x):
    total = x[0]
    for d in range(1, x.shape[0]):
        total = total + x[d]
    return group4(total)


def encode(x):
    power = x * x
    power = power * power
    power = power * power
    return jnp.where(x < 0, -power, power).astype(jnp.bfloat16)


def decode(code):
    power = code.astype(F32)
    fourth = lax.rsqrt(lax.rsqrt(jnp.maximum(jnp.abs(power), 2e-38)))
    root = fourth * lax.rsqrt(fourth)
    return jnp.where(power < 0, -root, root)


def stack_kernel(parts, g_ref, x_ref, pws_out, rob_out, tail_out,
                 recv, gv_ref, k_ref, xb_ref, x32_ref, st_ref, part_ref, inv_ref, coh_ref, wt_ref, share_ref, unit_ref,
                 pws_code, rob_code, tail_code,
                 g_sem, send_sem, recv_sems, out_sems, lag_sems, ring_sems, last_sems, pws_sems, tail_sems):
    me_d = lax.axis_index("day")
    me_l = lax.axis_index("lag")
    ndev, quads, here, lags = recv.shape[1:]
    rows = quads * here
    days = ndev * here
    width = lags // 4
    early = parts - 1
    fetch = pltpu.make_async_copy(g_ref, gv_ref, g_sem)
    fetch.start()
    entry_barrier(me_d, me_l)
    lanes = pl.ds(pl.multiple_of(me_l * width, width), width)

    def block(r, td, tl):
        return x_ref.at[pl.ds(((td * 4 + tl) * parts + r) * quads, quads)]

    for r in range(parts):
        def send(k, carry):
            td, tl = peer(k, me_d, me_l)
            pltpu.make_async_remote_copy(
                src_ref=block(r, td, tl),
                dst_ref=recv.at[r, me_d, :, :, lanes],
                send_sem=send_sem,
                recv_sem=recv_sems.at[r],
                device_id={"day": td, "lag": tl},
            ).start()
            return carry

        lax.fori_loop(1, 64, send, 0)
        pltpu.make_async_copy(block(r, me_d, me_l), recv.at[r, me_d, :, :, lanes], recv_sems.at[r]).start()

    fetch.wait()
    step = g_ref.shape[0]
    for i in range(lags // step):
        cut = i * step
        if cut:
            k_ref[cut:cut + step, :cut] = gv_ref[:, lags - cut:]
        k_ref[cut:cut + step, cut:] = gv_ref[:, :lags - cut]

    z, y = me_d // 4, lax.rem(me_d, 4)
    z_of = [lax.rem(z + k, 4) for k in range(4)]
    y_of = [lax.rem(y + k, 4) for k in range(4)]
    lag_peers = [lax.rem(me_l + k, 4) for k in (1, 2, 3)]
    z_peers = [{"day": z_of[k] * 4 + y, "lag": me_l} for k in (1, 3, 2)]
    y_peers = [{"day": z * 4 + y_of[k], "lag": me_l} for k in (1, 3, 2)]
    first, second = (z_peers, y_peers) * 2, (y_peers, z_peers) * 2
    codes, outs = (pws_code, rob_code) * 2, (pws_out, rob_out) * 2
    spans = (pl.ds(0, early - 1),) * 2 + (pl.ds(early - 1, 1),) * 2

    def push(i, src, dst, sem, to):
        pltpu.make_async_remote_copy(
            src_ref=src, dst_ref=dst, send_sem=out_sems.at[i], recv_sem=sem, device_id=to
        ).start()

    def to_lag_group(i):
        dst = outs[i].at[spans[i], me_d, me_l]
        for tl in lag_peers:
            push(i, codes[i].at[spans[i], tl], dst, lag_sems.at[i], {"day": me_d, "lag": tl})
        pltpu.make_async_copy(codes[i].at[spans[i], me_l], dst, lag_sems.at[i]).start()

    def to_rings(i):
        own = outs[i].at[spans[i], me_d]
        pltpu.make_async_copy(own, own, lag_sems.at[i]).wait()
        for n, to in enumerate(first[i]):
            push(i, own, own, ring_sems.at[i, n], to)
        for to in second[i]:
            push(i, own, own, last_sems.at[i], to)

    def forward(i, turns):
        for n in turns:
            k = (3, 1, 2)[n]
            day = (z_of[k] * 4 + y, z * 4 + y_of[k])[i % 2]
            got = outs[i].at[spans[i], day]
            pltpu.make_async_copy(got, got, ring_sems.at[i, n]).wait()
            for to in second[i]:
                push(i, got, got, last_sems.at[i], to)

    def finish(i):
        most = outs[i].at[spans[i], pl.ds(0, 12)]
        pltpu.make_async_copy(most, most, last_sems.at[i]).wait()
        for part in (outs[i].at[spans[i], pl.ds(0, 15)], codes[i].at[spans[i], pl.ds(0, 3)]):
            pltpu.make_async_copy(part, part, out_sems.at[i]).wait()

    def coded(slot):
        top = jnp.max(jnp.abs(st_ref[...]), axis=(0, 1), keepdims=True)
        top = jnp.maximum(top, 1e-30)
        unit_ref[slot] = jnp.broadcast_to(top / 16384.0, (1, 128))
        stack = st_ref[...]
        stack = jnp.concatenate([stack[j * here:j * here + 1] for j in range(quads)], axis=0)
        return encode(stack * (16384.0 / top))

    def one_part(r, hooks):
        hooks[0]()
        pltpu.make_async_copy(recv.at[r], recv.at[r], recv_sems.at[r]).wait()

        @pl.loop(0, ndev, unroll=2)
        def _(d):
            x = recv[r, d].reshape(rows, lags)
            xb_ref[d] = x
            data = x.astype(F32)
            x32_ref[d] = data
            part_ref[d] = fold(data * data)

        inv_ref[...] = 1.0 / jnp.sqrt(lane_sum(part_ref) / lags + EPS)
        hooks[1]()
        tile = 256

        def phase(t):
            at = pl.ds(pl.multiple_of(t * tile, tile), tile)
            quad = jnp.dot(xb_ref[...].reshape(ndev * rows, lags), k_ref[:, at], preferred_element_type=F32)
            lin = jnp.zeros((rows, tile), F32)
            csum = jnp.zeros((rows, tile), F32)
            ssum = jnp.zeros((rows, tile), F32)
            for d in range(ndev):
                data = x32_ref[d, :, at]
                q = quad[d * rows:(d + 1) * rows]
                scale = wide(inv_ref[d], tile)
                inv = jnp.minimum(lax.rsqrt(data * data + q * q), 10.0 * scale)
                lin = lin + data * scale
                csum = csum + data * inv
                ssum = ssum + q * inv
            csum = group4(csum)
            ssum = group4(ssum)
            st_ref[:, at] = group4(lin) / days * ((csum * csum + ssum * ssum) / (days * days))

        half = lags // tile // 2
        pl.loop(0, half, unroll=2)(phase)
        hooks[2]()
        pl.loop(half, 2 * half, unroll=2)(phase)
        code = coded(r)
        for j in range(4):
            pws_code[r, j] = code[:, j * width:(j + 1) * width]
        hooks[3]()
        for step in range(ITERS):
            stack = st_ref[...]
            msq = jnp.sum(fold(stack * stack), axis=1, keepdims=True) / lags
            st_ref[...] = stack * (1.0 / jnp.sqrt(msq + EPS))

            @pl.loop(0, ndev, unroll=4)
            def _(d):
                part_ref[d] = fold(x32_ref[d] * st_ref[...])

            coh_ref[...] = lane_sum(part_ref) * inv_ref[...] / lags

            @pl.loop(0, ndev, unroll=4)
            def _(d):
                diff = x32_ref[d] * wide(inv_ref[d], lags) - wide(coh_ref[d], lags) * st_ref[...]
                part_ref[d] = fold(diff * diff)

            res = lane_sum(part_ref) / lags
            rbar = day_sum(res) / days
            weight = (0.1 + jnp.abs(coh_ref[...])) / (res + rbar + EPS)
            total = day_sum(weight)
            wt_ref[...] = weight * inv_ref[...]
            chunk = 512

            @pl.loop(0, lags // chunk)
            def _(t):
                at = pl.ds(pl.multiple_of(t * chunk, chunk), chunk)
                mix = wide(wt_ref[0], chunk) * x32_ref[0, :, at]
                for d in range(1, ndev):
                    mix = mix + wide(wt_ref[d], chunk) * x32_ref[d, :, at]
                st_ref[:, at] = group4(mix)

            if step < ITERS - 1:
                hooks[4 + step]()
        st_ref[...] = st_ref[...] * wide(1.0 / total, lags)
        lane = lax.broadcasted_iota(jnp.int32, (rows, 128), 1)
        shares = jnp.zeros((rows, 128), F32)
        for d in range(ndev):
            shares = jnp.where(lane == d, weight[d] / total, shares)
        share_ref[pl.ds(pl.multiple_of(r * rows, rows), rows), :] = shares
        return coded(parts + r)

    def nothing():
        pass

    def each(action, items, *more):
        return lambda: [action(i, *more) for i in items]

    def early_part(r, hooks):
        code = one_part(r, hooks)
        for j in range(4):
            rob_code[r, j] = code[:, j * width:(j + 1) * width]

    pl.loop(0, early - 1)(lambda r: early_part(r, [nothing] * 6))
    early_part(early - 1, [each(to_lag_group, (0, 1)), nothing, nothing, nothing, nothing, each(to_rings, (0, 1))])

    def to_all(src, dst, sems):
        def send(k, carry):
            td, tl = peer(k, me_d, me_l)
            pltpu.make_async_remote_copy(
                src_ref=src(td, tl), dst_ref=dst, send_sem=sems.at[0], recv_sem=sems.at[1],
                device_id={"day": td, "lag": tl},
            ).start()
            return carry

        lax.fori_loop(1, 64, send, 0)
        pltpu.make_async_copy(src(me_d, me_l), dst, sems.at[1]).start()

    def last_pws():
        to_all(lambda td, tl: pws_code.at[early, tl], pws_out.at[early, me_d, me_l], pws_sems)

    def mid_phase():
        each(to_rings, (2, 3))()
        each(forward, (0, 1), (0, 1))()

    def after_phase():
        each(forward, (0, 1), (2,))()
        last_pws()

    code = one_part(early, [
        each(to_lag_group, (2, 3)), nothing, mid_phase, after_phase, each(forward, (2, 3), (0, 1)),
        each(forward, (2, 3), (2,))])

    lane = lax.broadcasted_iota(jnp.int32, (1, 128), 1)
    extra = jnp.zeros((1, 128), F32)
    for j in range(2 * parts):
        extra = jnp.where(lane == 64 + j, unit_ref[j], extra)
    row = lax.broadcasted_iota(jnp.int32, (here, 128), 0)
    words = share_ref[...].T[:ndev]
    words = jnp.where(lax.broadcasted_iota(jnp.int32, words.shape, 1) < 64, words, extra)
    high = words.astype(jnp.bfloat16).astype(F32)
    mid = (words - high).astype(jnp.bfloat16).astype(F32)
    low = words - high - mid
    for d in range(ndev):
        piece = jnp.where(row == 0, high[d:d + 1], jnp.where(row == 1, mid[d:d + 1], low[d:d + 1])).astype(jnp.bfloat16)
        for j in range(4):
            tail_code[d, j, :, :width] = code[:, j * width:(j + 1) * width]
            tail_code[d, j, :, width:] = piece

    to_all(lambda td, tl: tail_code.at[td, tl], tail_out.at[me_d, me_l], tail_sems)
    for r in range(parts):
        most = x_ref.at[pl.ds(0, 63 * quads)]
        pltpu.make_async_copy(most, most, send_sem).wait()
    for i in range(4):
        finish(i)
    last = pws_out.at[early]
    pltpu.make_async_copy(last, last, pws_sems.at[1]).wait()
    for part in (last.at[pl.ds(0, ndev - 1)], last.at[ndev - 1, pl.ds(0, 3)]):
        pltpu.make_async_copy(part, part, pws_sems.at[0]).wait()
    pltpu.make_async_copy(tail_out, tail_out, tail_sems.at[1]).wait()
    for part in (tail_code.at[pl.ds(0, ndev - 1)], tail_code.at[ndev - 1, pl.ds(0, 3)]):
        pltpu.make_async_copy(part, part, tail_sems.at[0]).wait()


def stacks(g, x):
    pairs, here, width = x.shape
    lags = 4 * width
    parts = 4
    quads = pairs // 64 // parts
    part = quads * here
    thin = pltpu.VMEM((16, part, 128), F32)
    dma = pltpu.SemaphoreType.DMA
    bf16 = jnp.bfloat16
    return pl.pallas_call(
        functools.partial(stack_kernel, parts),
        out_shape=(
            jax.ShapeDtypeStruct((parts, 16, 4, quads, width), bf16),
            jax.ShapeDtypeStruct((parts - 1, 16, 4, quads, width), bf16),
            jax.ShapeDtypeStruct((16, 4, quads, width + 128), bf16),
        ),
        in_specs=[HBM, HBM],
        out_specs=(HBM,) * 3,
        scratch_shapes=[
            pltpu.VMEM((parts, 16, quads, here, lags), x.dtype),
            pltpu.VMEM(g.shape, bf16),
            pltpu.VMEM((lags, lags), bf16),
            pltpu.VMEM((16, part, lags), bf16),
            pltpu.VMEM((16, part, lags), F32),
            pltpu.VMEM((part, lags), F32),
            thin, thin, thin, thin,
            pltpu.VMEM((128, 128), F32),
            pltpu.VMEM((2 * parts, 1, 128), F32),
            pltpu.VMEM((parts, 4, quads, width), bf16),
            pltpu.VMEM((parts - 1, 4, quads, width), bf16),
            pltpu.VMEM((16, 4, quads, width + 128), bf16),
            dma, dma, dma((parts,)), dma((4,)), dma((4,)), dma((4, 3)), dma((4,)), dma((2,)), dma((2,)),
        ],
        compiler_params=pltpu.CompilerParams(collective_id=0, has_side_effects=True, vmem_limit_bytes=63 * 2**20),
        name="stacks",
    )(g, x)


def decode_kernel(pws_ref, rob_ref, tail_ref, pws_out, rob_out, w_out, words_ref):
    step = pl.program_id(0)
    parts, here, _, quads, width = pws_ref.shape
    count = parts * quads
    lane = lax.broadcasted_iota(jnp.int32, (count, 128), 1)
    slot = lax.broadcasted_iota(jnp.int32, (count, 128), 0) // quads + 64
    for d in range(here):
        for l in range(4):
            c = d * 4 + l
            word = jnp.sum(tail_ref[d, l, :, width:].astype(F32)[:3], axis=0, keepdims=True)
            words_ref[step * here * 4 + c] = word
            units = []
            for base in (0, parts):
                units.append(jnp.sum(jnp.where(lane == slot + base, word, 0.0), axis=1, keepdims=True))
            at = slice(c * count, (c + 1) * count)
            pws_out[at, :] = decode(pws_ref[:, d, l].reshape(count, width)) * units[0]
            rob = [rob_ref[r, d, l].astype(F32) for r in range(parts - 1)] + [tail_ref[d, l, :, :width].astype(F32)]
            rob_out[at, :] = decode(jnp.concatenate(rob, axis=0)) * units[1]

    @pl.when(step == pl.num_programs(0) - 1)
    def _():
        words = words_ref[...].reshape(64, 128)
        source = lax.broadcasted_iota(jnp.int32, (128, 128), 0)
        target = lax.broadcasted_iota(jnp.int32, (128, 128), 1)
        row = lax.broadcasted_iota(jnp.int32, (64, 128), 0)
        mine = lax.broadcasted_iota(jnp.int32, (64, 128), 1) // 16 == row % 8
        for dd in range(w_out.shape[0]):
            pick = jnp.where(source == target % 16 * 4 + dd, 1.0, 0.0)
            moved = jnp.dot(words, pick, precision=lax.Precision.HIGHEST, preferred_element_type=F32)
            moved = jnp.where(mine, moved, 0.0)
            for j in range(8):
                w_out[dd:dd + 1, j * 128:(j + 1) * 128] = jnp.sum(moved[j * 8:j * 8 + 8], axis=0, keepdims=True)


def decoded(pws, rob, tail):
    parts, days, _, quads, width = pws.shape
    here = 4
    pairs = 64 * parts * quads
    count = pairs * here // days
    big = jax.ShapeDtypeStruct((pairs, width), F32)
    row = pl.BlockSpec((count, width), lambda i: (i, 0))
    return pl.pallas_call(
        decode_kernel,
        out_shape=(big, big, jax.ShapeDtypeStruct((4, pairs), F32)),
        grid=(days // here,),
        in_specs=[
            pl.BlockSpec((parts, here, 4, quads, width), lambda i: (0, i, 0, 0, 0)),
            pl.BlockSpec((parts - 1, here, 4, quads, width), lambda i: (0, i, 0, 0, 0)),
            pl.BlockSpec((here, 4, quads, width + 128), lambda i: (i, 0, 0, 0)),
        ],
        out_specs=(row, row, pl.BlockSpec((4, pairs), lambda i: (0, 0))),
        scratch_shapes=[pltpu.VMEM((64, 1, 128), F32)],
        compiler_params=pltpu.CompilerParams(vmem_limit_bytes=63 * 2**20),
        name="decoded",
    )(pws, rob, tail)


def per_device(corr):
    g = jnp.asarray(hilbert_rows(256, corr.shape[2] * 4))
    pws, rob, shares = decoded(*stacks(g, corr))
    return pws, rob, shares.T


def solution(mesh):
    return jax.shard_map(
        per_device,
        mesh=mesh,
        in_specs=(P("pair", "day", "lag"),),
        out_specs=(P("pair", "lag"), P("pair", "lag"), P("pair", "day")),
        check_vma=False,
    )
```

```python
import functools

import jax
import jax.numpy as jnp
import numpy as np
from jax import lax
from jax.experimental import pallas as pl
from jax.experimental.pallas import tpu as pltpu
from jax.sharding import PartitionSpec as P

ITERS = 3
EPS = 1e-06
HBM = pl.BlockSpec(memory_space=pl.ANY)
VMEM = pl.BlockSpec(memory_space=pltpu.VMEM)
F32 = jnp.float32


def hilbert_matrix(lags):
    offset = (np.arange(lags)[None, :] - np.arange(lags)[:, None]) % lags
    odd = offset % 2 == 1
    angle = np.pi * offset / lags
    value = np.where(odd, 2.0 / lags * np.cos(angle) / np.where(odd, np.sin(angle), 1.0), 0.0)
    return value.astype(np.float32).astype(jnp.bfloat16)


def peer(k, me_d, me_l):
    a = lax.rem(k, 4)
    z = lax.rem(me_d // 4 + a + k // 4, 4)
    y = lax.rem(lax.rem(me_d, 4) + a, 4)
    x = lax.rem(me_l // 2 + a + k // 16, 2)
    c = lax.rem(me_l + k // 32, 2)
    return z * 4 + y, x * 2 + c


def entry_barrier(d, l):
    barrier = pltpu.get_barrier_semaphore()

    def greet(k, carry):
        td, tl = peer(k, d, l)
        pl.semaphore_signal(barrier, inc=1, device_id={"day": td, "lag": tl})
        return carry

    lax.fori_loop(1, 64, greet, 0)
    pl.semaphore_wait(barrier, 63)


def group4(x):
    n = x.shape[0]
    row = lax.broadcasted_iota(jnp.int32, x.shape, 0)
    other = jnp.where(row % 2 == 0, pltpu.roll(x, n - 1, 0), pltpu.roll(x, 1, 0))
    x = x + other
    other = jnp.where(row % 4 < 2, pltpu.roll(x, n - 2, 0), pltpu.roll(x, 2, 0))
    return x + other


def wide(x, lanes):
    return jnp.concatenate([x] * (lanes // 128), axis=1)


def fold(x):
    total = x[:, :128]
    for j in range(128, x.shape[1], 128):
        total = total + x[:, j:j + 128]
    return total


def lane_sum(ref):
    ndev, rows, lanes = ref.shape
    total = jnp.sum(ref[...].reshape(ndev * rows, lanes), axis=1, keepdims=True)
    return jnp.broadcast_to(total, (ndev * rows, lanes)).reshape(ndev, rows, lanes)


def day_sum(x):
    total = x[0]
    for d in range(1, x.shape[0]):
        total = total + x[d]
    return group4(total)


def encode(x):
    power = x * x
    power = power * power
    power = power * power
    return jnp.where(x < 0, -power, power)


def decode(code):
    power = code.astype(F32)
    fourth = lax.rsqrt(lax.rsqrt(jnp.maximum(jnp.abs(power), 2e-38)))
    root = fourth * lax.rsqrt(fourth)
    return jnp.where(power < 0, -root, root)


def stack_kernel(parts, g_ref, x_ref, pws_out, rob_out, tail_out,
                 recv, k_ref, xb_ref, x32_ref, st_ref, part_ref, inv_ref, coh_ref, wt_ref, share_ref, unit_ref,
                 pws_code, rob_code, tail_code,
                 g_sem, send_sem, recv_sems, out_sems, lag_sems, ring_sems, last_sems, pws_sems, tail_sems):
    me_d = lax.axis_index("day")
    me_l = lax.axis_index("lag")
    ndev, quads, here, lags = recv.shape[1:]
    rows = quads * here
    days = ndev * here
    width = lags // 4
    early = parts - 1
    fetch = pltpu.make_async_copy(g_ref, k_ref, g_sem)
    fetch.start()
    entry_barrier(me_d, me_l)
    lanes = pl.ds(pl.multiple_of(me_l * width, width), width)

    def block(r, td, tl):
        return x_ref.at[pl.ds(((td * 4 + tl) * parts + r) * quads, quads)]

    for r in range(parts):
        def send(k, carry):
            td, tl = peer(k, me_d, me_l)
            pltpu.make_async_remote_copy(
                src_ref=block(r, td, tl),
                dst_ref=recv.at[r, me_d, :, :, lanes],
                send_sem=send_sem,
                recv_sem=recv_sems.at[r],
                device_id={"day": td, "lag": tl},
            ).start()
            return carry

        lax.fori_loop(1, 64, send, 0)
        pltpu.make_async_copy(block(r, me_d, me_l), recv.at[r, me_d, :, :, lanes], recv_sems.at[r]).start()

    fetch.wait()
    z, y = me_d // 4, lax.rem(me_d, 4)
    z_of = [lax.rem(z + k, 4) for k in range(4)]
    y_of = [lax.rem(y + k, 4) for k in range(4)]
    lag_peers = [lax.rem(me_l + k, 4) for k in (1, 2, 3)]
    z_peers = [{"day": z_of[k] * 4 + y, "lag": me_l} for k in (1, 3, 2)]
    y_peers = [{"day": z * 4 + y_of[k], "lag": me_l} for k in (1, 3, 2)]
    first, second = (z_peers, y_peers) * 2, (y_peers, z_peers) * 2
    codes, outs = (pws_code, rob_code) * 2, (pws_out, rob_out) * 2
    spans = (pl.ds(0, early - 1),) * 2 + (pl.ds(early - 1, 1),) * 2

    def push(i, src, dst, sem, to):
        pltpu.make_async_remote_copy(
            src_ref=src, dst_ref=dst, send_sem=out_sems.at[i], recv_sem=sem, device_id=to
        ).start()

    def to_lag_group(i):
        dst = outs[i].at[spans[i], me_d, me_l]
        for tl in lag_peers:
            push(i, codes[i].at[spans[i], tl], dst, lag_sems.at[i], {"day": me_d, "lag": tl})
        pltpu.make_async_copy(codes[i].at[spans[i], me_l], dst, lag_sems.at[i]).start()

    def to_rings(i):
        own = outs[i].at[spans[i], me_d]
        pltpu.make_async_copy(own, own, lag_sems.at[i]).wait()
        for n, to in enumerate(first[i]):
            push(i, own, own, ring_sems.at[i, n], to)
        for to in second[i]:
            push(i, own, own, last_sems.at[i], to)

    def forward(i, turns):
        for n in turns:
            k = (3, 1, 2)[n]
            day = (z_of[k] * 4 + y, z * 4 + y_of[k])[i % 2]
            got = outs[i].at[spans[i], day]
            pltpu.make_async_copy(got, got, ring_sems.at[i, n]).wait()
            for to in second[i]:
                push(i, got, got, last_sems.at[i], to)

    def finish(i):
        most = outs[i].at[spans[i], pl.ds(0, 12)]
        pltpu.make_async_copy(most, most, last_sems.at[i]).wait()
        for part in (outs[i].at[spans[i], pl.ds(0, 15)], codes[i].at[spans[i], pl.ds(0, 3)]):
            pltpu.make_async_copy(part, part, out_sems.at[i]).wait()

    def coded(slot):
        top = jnp.max(jnp.abs(st_ref[...]), axis=(0, 1), keepdims=True)
        top = jnp.maximum(top, 1e-30)
        unit_ref[slot] = jnp.broadcast_to(top / 16384.0, (1, 128))
        stack = st_ref[...]
        stack = jnp.concatenate([stack[j * here:j * here + 1] for j in range(quads)], axis=0)
        return encode(stack * (16384.0 / top))

    def as_tile(code, j):
        pieces = [code[:, t:t + 128] for t in range(j * width, (j + 1) * width, 128)]
        return jnp.concatenate(pieces, axis=0).astype(jnp.bfloat16)

    def one_part(r, hooks):
        hooks[0]()
        pltpu.make_async_copy(recv.at[r], recv.at[r], recv_sems.at[r]).wait()

        @pl.loop(0, ndev, unroll=2)
        def _(d):
            x = recv[r, d].reshape(rows, lags)
            xb_ref[d] = x
            data = x.astype(F32)
            x32_ref[d] = data
            part_ref[d] = fold(data * data)

        inv_ref[...] = 1.0 / jnp.sqrt(lane_sum(part_ref) / lags + EPS)
        hooks[1]()
        tile = 256

        def phase(t):
            at = pl.ds(pl.multiple_of(t * tile, tile), tile)
            quad = jnp.dot(xb_ref[...].reshape(ndev * rows, lags), k_ref[:, at], preferred_element_type=F32)
            lin = jnp.zeros((rows, tile), F32)
            csum = jnp.zeros((rows, tile), F32)
            ssum = jnp.zeros((rows, tile), F32)
            for d in range(ndev):
                data = x32_ref[d, :, at]
                q = quad[d * rows:(d + 1) * rows]
                scale = wide(inv_ref[d], tile)
                inv = jnp.minimum(lax.rsqrt(data * data + q * q), 10.0 * scale)
                lin = lin + data * scale
                csum = csum + data * inv
                ssum = ssum + q * inv
            csum = group4(csum)
            ssum = group4(ssum)
            st_ref[:, at] = group4(lin) / days * ((csum * csum + ssum * ssum) / (days * days))

        half = lags // tile // 2
        pl.loop(0, half, unroll=2)(phase)
        hooks[2]()
        pl.loop(half, 2 * half, unroll=2)(phase)
        code = coded(r)
        for j in range(4):
            pws_code[r, j] = as_tile(code, j)
        hooks[3]()
        for step in range(ITERS):
            stack = st_ref[...]
            msq = jnp.sum(fold(stack * stack), axis=1, keepdims=True) / lags
            st_ref[...] = stack * (1.0 / jnp.sqrt(msq + EPS))

            @pl.loop(0, ndev, unroll=4)
            def _(d):
                part_ref[d] = fold(x32_ref[d] * st_ref[...])

            coh_ref[...] = lane_sum(part_ref) * inv_ref[...] / lags

            @pl.loop(0, ndev, unroll=4)
            def _(d):
                diff = x32_ref[d] * wide(inv_ref[d], lags) - wide(coh_ref[d], lags) * st_ref[...]
                part_ref[d] = fold(diff * diff)

            res = lane_sum(part_ref) / lags
            rbar = day_sum(res) / days
            weight = (0.1 + jnp.abs(coh_ref[...])) / (res + rbar + EPS)
            total = day_sum(weight)
            wt_ref[...] = weight * inv_ref[...]
            chunk = 512

            @pl.loop(0, lags // chunk)
            def _(t):
                at = pl.ds(pl.multiple_of(t * chunk, chunk), chunk)
                mix = wide(wt_ref[0], chunk) * x32_ref[0, :, at]
                for d in range(1, ndev):
                    mix = mix + wide(wt_ref[d], chunk) * x32_ref[d, :, at]
                st_ref[:, at] = group4(mix)

            if step < ITERS - 1:
                hooks[4 + step]()
        st_ref[...] = st_ref[...] * wide(1.0 / total, lags)
        lane = lax.broadcasted_iota(jnp.int32, (rows, 128), 1)
        shares = jnp.zeros((rows, 128), F32)
        for d in range(ndev):
            shares = jnp.where(lane == d, weight[d] / total, shares)
        share_ref[pl.ds(pl.multiple_of(r * rows, rows), rows), :] = shares
        return coded(parts + r)

    def nothing():
        pass

    def each(action, items, *more):
        return lambda: [action(i, *more) for i in items]

    def early_part(r, hooks):
        code = one_part(r, hooks)
        for j in range(4):
            rob_code[r, j] = as_tile(code, j)

    pl.loop(0, early - 1)(lambda r: early_part(r, [nothing] * 6))
    early_part(early - 1, [each(to_lag_group, (0, 1)), nothing, nothing, nothing, nothing, each(to_rings, (0, 1))])

    def to_all(src, dst, sems):
        def send(k, carry):
            td, tl = peer(k, me_d, me_l)
            pltpu.make_async_remote_copy(
                src_ref=src(td, tl), dst_ref=dst, send_sem=sems.at[0], recv_sem=sems.at[1],
                device_id={"day": td, "lag": tl},
            ).start()
            return carry

        lax.fori_loop(1, 64, send, 0)
        pltpu.make_async_copy(src(me_d, me_l), dst, sems.at[1]).start()

    def last_pws():
        to_all(lambda td, tl: pws_code.at[early, tl], pws_out.at[early, me_d, me_l], pws_sems)

    def mid_phase():
        each(to_rings, (2, 3))()
        each(forward, (0, 1), (0, 1))()

    def after_phase():
        each(forward, (0, 1), (2,))()
        last_pws()

    code = one_part(early, [
        each(to_lag_group, (2, 3)), nothing, mid_phase, after_phase, each(forward, (2, 3), (0, 1)),
        each(forward, (2, 3), (2,))])

    lane = lax.broadcasted_iota(jnp.int32, (1, 128), 1)
    extra = jnp.zeros((1, 128), F32)
    for j in range(2 * parts):
        extra = jnp.where(lane == 64 + j, unit_ref[j], extra)
    row = lax.broadcasted_iota(jnp.int32, (here, 128), 0)
    words = share_ref[...].T[:ndev]
    words = jnp.where(lax.broadcasted_iota(jnp.int32, words.shape, 1) < 64, words, extra)
    high = words.astype(jnp.bfloat16).astype(F32)
    mid = (words - high).astype(jnp.bfloat16).astype(F32)
    low = words - high - mid
    for d in range(ndev):
        piece = jnp.where(row == 0, high[d:d + 1], jnp.where(row == 1, mid[d:d + 1], low[d:d + 1])).astype(jnp.bfloat16)
        for j in range(4):
            tail_code[d, j, :, :width] = code[:, j * width:(j + 1) * width].astype(jnp.bfloat16)
            tail_code[d, j, :, width:] = piece

    to_all(lambda td, tl: tail_code.at[td, tl], tail_out.at[me_d, me_l], tail_sems)
    for r in range(parts):
        most = x_ref.at[pl.ds(0, 63 * quads)]
        pltpu.make_async_copy(most, most, send_sem).wait()
    for i in range(4):
        finish(i)
    last = pws_out.at[early]
    pltpu.make_async_copy(last, last, pws_sems.at[1]).wait()
    for part in (last.at[pl.ds(0, ndev - 1)], last.at[ndev - 1, pl.ds(0, 3)]):
        pltpu.make_async_copy(part, part, pws_sems.at[0]).wait()
    pltpu.make_async_copy(tail_out, tail_out, tail_sems.at[1]).wait()
    for part in (tail_code.at[pl.ds(0, ndev - 1)], tail_code.at[ndev - 1, pl.ds(0, 3)]):
        pltpu.make_async_copy(part, part, tail_sems.at[0]).wait()


def stacks(g, x):
    pairs, here, width = x.shape
    lags = 4 * width
    parts = 4
    quads = pairs // 64 // parts
    part = quads * here
    tile = (quads * width // 128, 128)
    thin = pltpu.VMEM((16, part, 128), F32)
    dma = pltpu.SemaphoreType.DMA
    bf16 = jnp.bfloat16
    return pl.pallas_call(
        functools.partial(stack_kernel, parts),
        out_shape=(
            jax.ShapeDtypeStruct((parts, 16, 4) + tile, bf16),
            jax.ShapeDtypeStruct((parts - 1, 16, 4) + tile, bf16),
            jax.ShapeDtypeStruct((16, 4, quads, width + 128), bf16),
        ),
        in_specs=[HBM, HBM],
        out_specs=(VMEM,) * 3,
        scratch_shapes=[
            pltpu.VMEM((parts, 16, quads, here, lags), x.dtype),
            pltpu.VMEM(g.shape, bf16),
            pltpu.VMEM((16, part, lags), bf16),
            pltpu.VMEM((16, part, lags), F32),
            pltpu.VMEM((part, lags), F32),
            thin, thin, thin, thin,
            pltpu.VMEM((128, 128), F32),
            pltpu.VMEM((2 * parts, 1, 128), F32),
            pltpu.VMEM((parts, 4) + tile, bf16),
            pltpu.VMEM((parts - 1, 4) + tile, bf16),
            pltpu.VMEM((16, 4, quads, width + 128), bf16),
            dma, dma, dma((parts,)), dma((4,)), dma((4,)), dma((4, 3)), dma((4,)), dma((2,)), dma((2,)),
        ],
        compiler_params=pltpu.CompilerParams(collective_id=0, has_side_effects=True, vmem_limit_bytes=50 * 2**20),
        name="stacks",
    )(g, x)


def decode_kernel(pws_ref, rob_ref, tail_ref, pws_out, rob_out, w_out, words_ref):
    step = pl.program_id(0)
    _, _, quads, width = tail_ref.shape
    width -= 128
    here = 4
    parts = pws_ref.shape[0]
    for d in range(here):
        for l in range(4):
            c = d * 4 + l
            word = jnp.sum(tail_ref[step * here + d, l, :, width:].astype(F32)[:3], axis=0, keepdims=True)
            words_ref[step * here * 4 + c] = word
            for r in range(parts):
                at = slice((c * parts + r) * quads, (c * parts + r + 1) * quads)
                for ref, out, slot in ((pws_ref, pws_out, 64 + r), (rob_ref, rob_out, 64 + parts + r)):
                    unit = word[:, slot:slot + 1]
                    if r == ref.shape[0]:
                        out[at, :] = decode(tail_ref[step * here + d, l, :, :width]) * unit
                        continue
                    x = decode(ref[r, step * here + d, l]) * unit
                    for t in range(width // 128):
                        out[at, t * 128:(t + 1) * 128] = x[t * quads:(t + 1) * quads]

    @pl.when(step == pl.num_programs(0) - 1)
    def _():
        words = words_ref[...].reshape(64, 128)
        source = lax.broadcasted_iota(jnp.int32, (128, 128), 0)
        target = lax.broadcasted_iota(jnp.int32, (128, 128), 1)
        row = lax.broadcasted_iota(jnp.int32, (64, 128), 0)
        mine = lax.broadcasted_iota(jnp.int32, (64, 128), 1) // 16 == row % 8
        for dd in range(w_out.shape[0]):
            pick = jnp.where(source == target % 16 * 4 + dd, 1.0, 0.0)
            moved = jnp.dot(words, pick, precision=lax.Precision.HIGHEST, preferred_element_type=F32)
            moved = jnp.where(mine, moved, 0.0)
            for j in range(8):
                w_out[dd:dd + 1, j * 128:(j + 1) * 128] = jnp.sum(moved[j * 8:j * 8 + 8], axis=0, keepdims=True)


def decoded(pws, rob, tail):
    parts, days = pws.shape[:2]
    quads, width = tail.shape[2], tail.shape[3] - 128
    here = 4
    pairs = 64 * parts * quads
    count = pairs * here // days
    big = jax.ShapeDtypeStruct((pairs, width), F32)
    row = pl.BlockSpec((count, width), lambda i: (i, 0))
    return pl.pallas_call(
        decode_kernel,
        out_shape=(big, big, jax.ShapeDtypeStruct((4, pairs), F32)),
        grid=(days // here,),
        in_specs=[VMEM] * 3,
        out_specs=(row, row, pl.BlockSpec((4, pairs), lambda i: (0, 0))),
        scratch_shapes=[pltpu.VMEM((64, 1, 128), F32)],
        compiler_params=pltpu.CompilerParams(vmem_limit_bytes=40 * 2**20),
        name="decoded",
    )(pws, rob, tail)


def per_device(corr):
    g = jnp.asarray(hilbert_matrix(corr.shape[2] * 4))
    pws, rob, shares = decoded(*stacks(g, corr))
    return pws, rob, shares.T


def solution(mesh):
    return jax.shard_map(
        per_device,
        mesh=mesh,
        in_specs=(P("pair", "day", "lag"),),
        out_specs=(P("pair", "lag"), P("pair", "lag"), P("pair", "day")),
        check_vma=False,
    )
```

```python
import functools

import jax
import jax.numpy as jnp
import numpy as np
from jax import lax
from jax.experimental import pallas as pl
from jax.experimental.pallas import tpu as pltpu
from jax.sharding import PartitionSpec as P

ITERS = 3
EPS = 1e-06
HBM = pl.BlockSpec(memory_space=pl.ANY)
VMEM = pl.BlockSpec(memory_space=pltpu.VMEM)
F32 = jnp.float32


def hilbert_matrix(lags):
    offset = (np.arange(lags)[None, :] - np.arange(lags)[:, None]) % lags
    odd = offset % 2 == 1
    angle = np.pi * offset / lags
    value = np.where(odd, 2.0 / lags * np.cos(angle) / np.where(odd, np.sin(angle), 1.0), 0.0)
    return value.astype(np.float32).astype(jnp.bfloat16)


def peer(k, me_d, me_l):
    a = lax.rem(k, 4)
    z = lax.rem(me_d // 4 + a + k // 4, 4)
    y = lax.rem(lax.rem(me_d, 4) + a, 4)
    x = lax.rem(me_l // 2 + a + k // 16, 2)
    c = lax.rem(me_l + k // 32, 2)
    return z * 4 + y, x * 2 + c


def entry_barrier(d, l):
    barrier = pltpu.get_barrier_semaphore()

    def greet(k, carry):
        td, tl = peer(k, d, l)
        pl.semaphore_signal(barrier, inc=1, device_id={"day": td, "lag": tl})
        return carry

    lax.fori_loop(1, 64, greet, 0)
    pl.semaphore_wait(barrier, 63)


def group4(x):
    n = x.shape[0]
    row = lax.broadcasted_iota(jnp.int32, x.shape, 0)
    other = jnp.where(row % 2 == 0, pltpu.roll(x, n - 1, 0), pltpu.roll(x, 1, 0))
    x = x + other
    other = jnp.where(row % 4 < 2, pltpu.roll(x, n - 2, 0), pltpu.roll(x, 2, 0))
    return x + other


def wide(x, lanes):
    return jnp.concatenate([x] * (lanes // 128), axis=1)


def fold(x):
    total = x[:, :128]
    for j in range(128, x.shape[1], 128):
        total = total + x[:, j:j + 128]
    return total


def lane_sum(ref):
    ndev, rows, lanes = ref.shape
    total = jnp.sum(ref[...].reshape(ndev * rows, lanes), axis=1, keepdims=True)
    return jnp.broadcast_to(total, (ndev * rows, lanes)).reshape(ndev, rows, lanes)


def day_sum(x):
    total = x[0]
    for d in range(1, x.shape[0]):
        total = total + x[d]
    return group4(total)


def encode(x):
    power = x * x
    power = power * power
    power = power * power
    return jnp.where(x < 0, -power, power)


def decode(code):
    power = code.astype(F32)
    fourth = lax.rsqrt(lax.rsqrt(jnp.maximum(jnp.abs(power), 2e-38)))
    root = fourth * lax.rsqrt(fourth)
    return jnp.where(power < 0, -root, root)


def stack_kernel(parts, g_ref, x_ref, pws_out, rob_out, tail_out,
                 recv, k_ref, xb_ref, x32_ref, st_ref, part_ref, inv_ref, coh_ref, wt_ref, share_ref, unit_ref,
                 pws_code, rob_code, tail_code,
                 g_sem, send_sem, recv_sems, out_sems, lag_sems, ring_sems, last_sems, pws_sems, tail_sems):
    me_d = lax.axis_index("day")
    me_l = lax.axis_index("lag")
    ndev, quads, here, lags = recv.shape[1:]
    rows = quads * here
    days = ndev * here
    width = lags // 4
    early = parts - 1
    fetch = pltpu.make_async_copy(g_ref, k_ref, g_sem)
    fetch.start()
    entry_barrier(me_d, me_l)
    lanes = pl.ds(pl.multiple_of(me_l * width, width), width)

    def block(r, td, tl):
        return x_ref.at[pl.ds(((td * 4 + tl) * parts + r) * quads, quads)]

    for r in range(parts):
        def send(k, carry):
            td, tl = peer(k, me_d, me_l)
            pltpu.make_async_remote_copy(
                src_ref=block(r, td, tl),
                dst_ref=recv.at[r, me_d, :, :, lanes],
                send_sem=send_sem,
                recv_sem=recv_sems.at[r],
                device_id={"day": td, "lag": tl},
            ).start()
            return carry

        lax.fori_loop(1, 64, send, 0)
        pltpu.make_async_copy(block(r, me_d, me_l), recv.at[r, me_d, :, :, lanes], recv_sems.at[r]).start()

    fetch.wait()
    z, y = me_d // 4, lax.rem(me_d, 4)
    z_of = [lax.rem(z + k, 4) for k in range(4)]
    y_of = [lax.rem(y + k, 4) for k in range(4)]
    lag_peers = [lax.rem(me_l + k, 4) for k in (1, 2, 3)]
    z_peers = [{"day": z_of[k] * 4 + y, "lag": me_l} for k in (1, 3, 2)]
    y_peers = [{"day": z * 4 + y_of[k], "lag": me_l} for k in (1, 3, 2)]
    first, second = (z_peers, y_peers) * 2, (y_peers, z_peers) * 2
    codes, outs = (pws_code, rob_code) * 2, (pws_out, rob_out) * 2
    spans = (pl.ds(0, early - 1),) * 2 + (pl.ds(early - 1, 1),) * 2

    def push(i, src, dst, sem, to):
        pltpu.make_async_remote_copy(
            src_ref=src, dst_ref=dst, send_sem=out_sems.at[i], recv_sem=sem, device_id=to
        ).start()

    def to_lag_group(i):
        dst = outs[i].at[spans[i], me_d, me_l]
        for tl in lag_peers:
            push(i, codes[i].at[spans[i], tl], dst, lag_sems.at[i], {"day": me_d, "lag": tl})
        pltpu.make_async_copy(codes[i].at[spans[i], me_l], dst, lag_sems.at[i]).start()

    def to_rings(i):
        own = outs[i].at[spans[i], me_d]
        pltpu.make_async_copy(own, own, lag_sems.at[i]).wait()
        for n, to in enumerate(first[i]):
            push(i, own, own, ring_sems.at[i, n], to)
        for to in second[i]:
            push(i, own, own, last_sems.at[i], to)

    def forward(i, turns):
        for n in turns:
            k = (3, 1, 2)[n]
            day = (z_of[k] * 4 + y, z * 4 + y_of[k])[i % 2]
            got = outs[i].at[spans[i], day]
            pltpu.make_async_copy(got, got, ring_sems.at[i, n]).wait()
            for to in second[i]:
                push(i, got, got, last_sems.at[i], to)

    def finish(i):
        most = outs[i].at[spans[i], pl.ds(0, 12)]
        pltpu.make_async_copy(most, most, last_sems.at[i]).wait()
        for part in (outs[i].at[spans[i], pl.ds(0, 15)], codes[i].at[spans[i], pl.ds(0, 3)]):
            pltpu.make_async_copy(part, part, out_sems.at[i]).wait()

    def coded(slot):
        top = jnp.max(jnp.abs(st_ref[...]), axis=(0, 1), keepdims=True)
        top = jnp.maximum(top, 1e-30)
        unit_ref[slot] = jnp.broadcast_to(top / 16384.0, (1, 128))
        stack = st_ref[...]
        stack = jnp.concatenate([stack[j * here:j * here + 1] for j in range(quads)], axis=0)
        return encode(stack * (16384.0 / top))

    def as_tile(code, j):
        pieces = [code[:, t:t + 128] for t in range(j * width, (j + 1) * width, 128)]
        return jnp.concatenate(pieces, axis=0).astype(jnp.bfloat16)

    def one_part(r, hooks):
        hooks[0]()
        pltpu.make_async_copy(recv.at[r], recv.at[r], recv_sems.at[r]).wait()

        @pl.loop(0, ndev, unroll=4)
        def _(d):
            x = recv[r, d].reshape(rows, lags)
            xb_ref[d] = x
            data = x.astype(F32)
            x32_ref[d] = data
            part_ref[d] = fold(data * data)

        inv_ref[...] = 1.0 / jnp.sqrt(lane_sum(part_ref) / lags + EPS)
        hooks[1]()
        tile = 256

        def phase(t):
            at = pl.ds(pl.multiple_of(t * tile, tile), tile)
            quad = jnp.dot(xb_ref[...].reshape(ndev * rows, lags), k_ref[:, at], preferred_element_type=F32)
            lin = jnp.zeros((rows, tile), F32)
            csum = jnp.zeros((rows, tile), F32)
            ssum = jnp.zeros((rows, tile), F32)
            for d in range(ndev):
                data = x32_ref[d, :, at]
                q = quad[d * rows:(d + 1) * rows]
                scale = wide(inv_ref[d], tile)
                inv = jnp.minimum(lax.rsqrt(data * data + q * q), 10.0 * scale)
                lin = lin + data * scale
                csum = csum + data * inv
                ssum = ssum + q * inv
            csum = group4(csum)
            ssum = group4(ssum)
            st_ref[:, at] = group4(lin) / days * ((csum * csum + ssum * ssum) / (days * days))

        half = lags // tile // 2
        pl.loop(0, half, unroll=4)(phase)
        hooks[2]()
        pl.loop(half, 2 * half, unroll=4)(phase)
        code = coded(r)
        for j in range(4):
            pws_code[r, j] = as_tile(code, j)
        hooks[3]()
        for step in range(ITERS):
            stack = st_ref[...]
            msq = jnp.sum(fold(stack * stack), axis=1, keepdims=True) / lags
            st_ref[...] = stack * (1.0 / jnp.sqrt(msq + EPS))

            @pl.loop(0, ndev, unroll=4)
            def _(d):
                part_ref[d] = fold(x32_ref[d] * st_ref[...])

            coh_ref[...] = lane_sum(part_ref) * inv_ref[...] / lags

            @pl.loop(0, ndev, unroll=4)
            def _(d):
                diff = x32_ref[d] * wide(inv_ref[d], lags) - wide(coh_ref[d], lags) * st_ref[...]
                part_ref[d] = fold(diff * diff)

            res = lane_sum(part_ref) / lags
            rbar = day_sum(res) / days
            weight = (0.1 + jnp.abs(coh_ref[...])) / (res + rbar + EPS)
            total = day_sum(weight)
            wt_ref[...] = weight * inv_ref[...]
            chunk = 512

            @pl.loop(0, lags // chunk)
            def _(t):
                at = pl.ds(pl.multiple_of(t * chunk, chunk), chunk)
                mix = wide(wt_ref[0], chunk) * x32_ref[0, :, at]
                for d in range(1, ndev):
                    mix = mix + wide(wt_ref[d], chunk) * x32_ref[d, :, at]
                st_ref[:, at] = group4(mix)

            if step < ITERS - 1:
                hooks[4 + step]()
        st_ref[...] = st_ref[...] * wide(1.0 / total, lags)
        lane = lax.broadcasted_iota(jnp.int32, (rows, 128), 1)
        shares = jnp.zeros((rows, 128), F32)
        for d in range(ndev):
            shares = jnp.where(lane == d, weight[d] / total, shares)
        share_ref[pl.ds(pl.multiple_of(r * rows, rows), rows), :] = shares
        return coded(parts + r)

    def nothing():
        pass

    def each(action, items, *more):
        return lambda: [action(i, *more) for i in items]

    def early_part(r, hooks):
        code = one_part(r, hooks)
        for j in range(4):
            rob_code[r, j] = as_tile(code, j)

    pl.loop(0, early - 1)(lambda r: early_part(r, [nothing] * 6))
    early_part(early - 1, [each(to_lag_group, (0, 1)), nothing, nothing, nothing, nothing, each(to_rings, (0, 1))])

    def to_all(src, dst, sems):
        def send(k, carry):
            td, tl = peer(k, me_d, me_l)
            pltpu.make_async_remote_copy(
                src_ref=src(td, tl), dst_ref=dst, send_sem=sems.at[0], recv_sem=sems.at[1],
                device_id={"day": td, "lag": tl},
            ).start()
            return carry

        lax.fori_loop(1, 64, send, 0)
        pltpu.make_async_copy(src(me_d, me_l), dst, sems.at[1]).start()

    def last_pws():
        to_all(lambda td, tl: pws_code.at[early, tl], pws_out.at[early, me_d, me_l], pws_sems)

    def mid_phase():
        each(to_rings, (2, 3))()
        each(forward, (0, 1), (0, 1))()

    def after_phase():
        last_pws()
        each(forward, (0, 1), (2,))()

    code = one_part(early, [
        each(to_lag_group, (2, 3)), nothing, mid_phase, after_phase, each(forward, (2, 3), (0, 1)),
        each(forward, (2, 3), (2,))])

    lane = lax.broadcasted_iota(jnp.int32, (1, 128), 1)
    extra = jnp.zeros((1, 128), F32)
    for j in range(2 * parts):
        extra = jnp.where(lane == 64 + j, unit_ref[j], extra)
    row = lax.broadcasted_iota(jnp.int32, (here, 128), 0)
    words = share_ref[...].T[:ndev]
    words = jnp.where(lax.broadcasted_iota(jnp.int32, words.shape, 1) < 64, words, extra)
    high = words.astype(jnp.bfloat16).astype(F32)
    mid = (words - high).astype(jnp.bfloat16).astype(F32)
    low = words - high - mid
    for d in range(ndev):
        piece = jnp.where(row == 0, high[d:d + 1], jnp.where(row == 1, mid[d:d + 1], low[d:d + 1])).astype(jnp.bfloat16)
        for j in range(4):
            tail_code[d, j, :, :width] = code[:, j * width:(j + 1) * width].astype(jnp.bfloat16)
            tail_code[d, j, :, width:] = piece

    to_all(lambda td, tl: tail_code.at[td, tl], tail_out.at[me_d, me_l], tail_sems)
    for r in range(parts):
        most = x_ref.at[pl.ds(0, 63 * quads)]
        pltpu.make_async_copy(most, most, send_sem).wait()
    for i in range(4):
        finish(i)
    last = pws_out.at[early]
    pltpu.make_async_copy(last, last, pws_sems.at[1]).wait()
    for part in (last.at[pl.ds(0, ndev - 1)], last.at[ndev - 1, pl.ds(0, 3)]):
        pltpu.make_async_copy(part, part, pws_sems.at[0]).wait()
    pltpu.make_async_copy(tail_out, tail_out, tail_sems.at[1]).wait()
    for part in (tail_code.at[pl.ds(0, ndev - 1)], tail_code.at[ndev - 1, pl.ds(0, 3)]):
        pltpu.make_async_copy(part, part, tail_sems.at[0]).wait()


def stacks(g, x):
    pairs, here, width = x.shape
    lags = 4 * width
    parts = 4
    quads = pairs // 64 // parts
    part = quads * here
    tile = (quads * width // 128, 128)
    thin = pltpu.VMEM((16, part, 128), F32)
    dma = pltpu.SemaphoreType.DMA
    bf16 = jnp.bfloat16
    return pl.pallas_call(
        functools.partial(stack_kernel, parts),
        out_shape=(
            jax.ShapeDtypeStruct((parts, 16, 4) + tile, bf16),
            jax.ShapeDtypeStruct((parts - 1, 16, 4) + tile, bf16),
            jax.ShapeDtypeStruct((16, 4, quads, width + 128), bf16),
        ),
        in_specs=[HBM, HBM],
        out_specs=(VMEM,) * 3,
        scratch_shapes=[
            pltpu.VMEM((parts, 16, quads, here, lags), x.dtype),
            pltpu.VMEM(g.shape, bf16),
            pltpu.VMEM((16, part, lags), bf16),
            pltpu.VMEM((16, part, lags), F32),
            pltpu.VMEM((part, lags), F32),
            thin, thin, thin, thin,
            pltpu.VMEM((128, 128), F32),
            pltpu.VMEM((2 * parts, 1, 128), F32),
            pltpu.VMEM((parts, 4) + tile, bf16),
            pltpu.VMEM((parts - 1, 4) + tile, bf16),
            pltpu.VMEM((16, 4, quads, width + 128), bf16),
            dma, dma, dma((parts,)), dma((4,)), dma((4,)), dma((4, 3)), dma((4,)), dma((2,)), dma((2,)),
        ],
        compiler_params=pltpu.CompilerParams(collective_id=0, has_side_effects=True, vmem_limit_bytes=50 * 2**20),
        name="stacks",
    )(g, x)


def decode_kernel(pws_ref, rob_ref, tail_ref, pws_out, rob_out, w_out, words_ref):
    step = pl.program_id(0)
    _, _, quads, width = tail_ref.shape
    width -= 128
    here = 4
    parts = pws_ref.shape[0]
    for d in range(here):
        for l in range(4):
            c = d * 4 + l
            word = jnp.sum(tail_ref[step * here + d, l, :, width:].astype(F32)[:3], axis=0, keepdims=True)
            words_ref[step * here * 4 + c] = word
            for r in range(parts):
                at = slice((c * parts + r) * quads, (c * parts + r + 1) * quads)
                for ref, out, slot in ((pws_ref, pws_out, 64 + r), (rob_ref, rob_out, 64 + parts + r)):
                    unit = word[:, slot:slot + 1]
                    if r == ref.shape[0]:
                        out[at, :] = decode(tail_ref[step * here + d, l, :, :width]) * unit
                        continue
                    x = decode(ref[r, step * here + d, l]) * unit
                    for t in range(width // 128):
                        out[at, t * 128:(t + 1) * 128] = x[t * quads:(t + 1) * quads]

    @pl.when(step == pl.num_programs(0) - 1)
    def _():
        words = words_ref[...].reshape(64, 128)
        source = lax.broadcasted_iota(jnp.int32, (128, 128), 0)
        target = lax.broadcasted_iota(jnp.int32, (128, 128), 1)
        row = lax.broadcasted_iota(jnp.int32, (64, 128), 0)
        mine = lax.broadcasted_iota(jnp.int32, (64, 128), 1) // 16 == row % 8
        for dd in range(w_out.shape[0]):
            pick = jnp.where(source == target % 16 * 4 + dd, 1.0, 0.0)
            moved = jnp.dot(words, pick, precision=lax.Precision.HIGHEST, preferred_element_type=F32)
            moved = jnp.where(mine, moved, 0.0)
            for j in range(8):
                w_out[dd:dd + 1, j * 128:(j + 1) * 128] = jnp.sum(moved[j * 8:j * 8 + 8], axis=0, keepdims=True)


def decoded(pws, rob, tail):
    parts, days = pws.shape[:2]
    quads, width = tail.shape[2], tail.shape[3] - 128
    here = 4
    pairs = 64 * parts * quads
    count = pairs * here // days
    big = jax.ShapeDtypeStruct((pairs, width), F32)
    row = pl.BlockSpec((count, width), lambda i: (i, 0))
    return pl.pallas_call(
        decode_kernel,
        out_shape=(big, big, jax.ShapeDtypeStruct((4, pairs), F32)),
        grid=(days // here,),
        in_specs=[VMEM] * 3,
        out_specs=(row, row, pl.BlockSpec((4, pairs), lambda i: (0, 0))),
        scratch_shapes=[pltpu.VMEM((64, 1, 128), F32)],
        compiler_params=pltpu.CompilerParams(vmem_limit_bytes=40 * 2**20),
        name="decoded",
    )(pws, rob, tail)


def per_device(corr):
    g = jnp.asarray(hilbert_matrix(corr.shape[2] * 4))
    pws, rob, shares = decoded(*stacks(g, corr))
    return pws, rob, shares.T


def solution(mesh):
    return jax.shard_map(
        per_device,
        mesh=mesh,
        in_specs=(P("pair", "day", "lag"),),
        out_specs=(P("pair", "lag"), P("pair", "lag"), P("pair", "day")),
        check_vma=False,
    )
```
